128 devices in a mesh: dp: 2 (over core), seq: 16 (over z, y), tensor: 4 (over x).
Axes of the slice: x: 4, y: 4, z: 4, core: 2. Of those that a mesh axis runs over, the one named last changes fastest.
Arguments:
- tokens: bfloat16 [16384, 3072], P(('dp', 'seq'), 'tensor'), parts along dimension 0, may hold values from -6 to 6
- w_qkv: bfloat16 [3072, 3, 4096], P(None, None, 'tensor'), may hold values from -0.109375 to 0.109375
- log_decay: float32 [32, 16384], P('tensor', ('dp', 'seq')), parts along dimension 1, as said below
- w_out: bfloat16 [4096, 3072], P('tensor'), may hold values from -0.125 to 0.125
Outputs:
- mixed: bfloat16 [16384, 3072], P(('dp', 'seq'), 'tensor'), parts along dimension 0
The draws below stay inside these ranges and needn't reach their ends.
There are 2 independent parts, one for each index of `dp`. The reference program is written for one: setup_inputs(seed, part) draws one part's arguments, and reference() takes and returns one part's arrays. A program takes and returns all parts, laid end to end along the dimension named above; an argument that names none is the same for every part. Nothing has to cross between parts.
Inputs may be any that keep to these rules, and one draw needn't show every extreme that they name: `log_decay`: every entry is at most 0.
All inputs are finite; a program needn't handle non-finite values.
Results may differ from the reference program's by a relative error of at most 0.017.
Values may be sent and summed in bfloat16 or wider, within the bound.
No kernel may reach another device: no remote copies, remote signals or barrier semaphores. Data moves between devices by JAX's collectives and lax.ppermute only.
A program may use at most 128 MiB of HBM per device.

```python
import math
import jax
import jax.numpy as jnp
from jax import lax

D = 3072
HDIM = 128
H_DEV = 8
TOK_DEV = 512
BLK = 512
HEADS = 32
TOKENS = 8192
N_SEQ = 16
N_TENSOR = 4


def draw_log_decay(key, part):
    key = jax.random.fold_in(key, 7)
    keys_all = jax.random.split(key, 8)
    fast_share = 0.2
    middle_share = 0.3
    classes = jax.random.uniform(keys_all[0], (HEADS,))
    fast_rates = jax.random.uniform(keys_all[1], (HEADS,), minval=1.0 / 50.0, maxval=1.0 / 30.0)
    middle_rates = jax.random.uniform(keys_all[2], (HEADS,), minval=0.25, maxval=1.0) / TOK_DEV
    slow_rates = jax.random.uniform(keys_all[3], (HEADS,), minval=0.1, maxval=0.3) / TOKENS
    attenuation_speeds = jnp.where(classes < fast_share, fast_rates, jnp.where(classes < fast_share + middle_share, middle_rates, slow_rates))
    rough_approximation = jax.random.uniform(keys_all[4], (HEADS, TOKENS), minval=0.5, maxval=1.5)
    division_factor = jax.random.uniform(keys_all[5], (HEADS, N_SEQ), minval=0.5, maxval=1.5)
    division_factor = jnp.repeat(division_factor, TOK_DEV, axis=1)
    spots = jax.random.randint(keys_all[6], (HEADS, 3), 0, TOKENS)
    discarded_elements = jax.random.uniform(keys_all[7], (HEADS, 3), minval=math.log(0.6), maxval=math.log(0.8))
    placement_sequence = jnp.arange(TOKENS)[None, None, :] == spots[:, :, None]
    spike_occurrences = jnp.sum(jnp.where(placement_sequence, discarded_elements[:, :, None], 0.0), axis=1)
    return (-(attenuation_speeds[:, None] * rough_approximation * division_factor) + spike_occurrences).astype(jnp.float32)


def spiked(values, own_key, source, target, shards_of, factor):
    def block_of(position):
        return (jnp.arange(values.shape[position]) // (values.shape[position] // shards_of)).reshape((-1,) + (1,) * (values.ndim - 1 - position))

    near = jax.random.permutation(own_key, shards_of)[block_of(target)]
    far = (block_of(target) + shards_of // 2) % shards_of
    return jnp.where((block_of(source) == near) | (block_of(source) == far), factor * values, values)


def shard_levels(key, shape, pieces, least, top_value):
    gain = 1.0
    for position, blocks in pieces:
        steps = jax.random.uniform(jax.random.fold_in(jax.random.fold_in(key, 6), position), (blocks,), jnp.float32, least / len(pieces), top_value / len(pieces))
        gain = gain * jnp.repeat(jnp.exp(steps), shape[position] // blocks).reshape((-1,) + (1,) * (len(shape) - 1 - position))
    return gain


def gaussian(stream_key, dims, scale, limit, cuts=(), kind=jnp.bfloat16):
    values = scale * jax.random.normal(stream_key, dims, jnp.float32)
    if cuts:
        values = values * shard_levels(stream_key, dims, cuts, -0.22, 0.18)
    return jnp.clip(values, -limit, limit).astype(kind)


def heavy_noise(stream_key, dims, scale, limit, shards, heavy, kind=jnp.bfloat16):
    values = scale * jax.random.normal(stream_key, dims, jnp.float32)
    if shards:
        values = values * shard_levels(stream_key, dims, shards, -0.22, 0.18)
    return jnp.clip(spiked(values, jax.random.fold_in(stream_key, 3), *heavy), -limit, limit).astype(kind)


def setup_inputs(seed: int = 0, part: int = 0) -> dict:
    seeds = jax.random.split(jax.random.key(seed), 5)
    part_keys = jax.random.split(jax.random.fold_in(seeds[4], part), 5)
    tokens = gaussian(part_keys[0], (TOKENS, D), 1.0, 6.0, ((0, 16), (1, 4)))
    w_qkv = gaussian(seeds[1], (D, 3, HEADS * HDIM), D ** -0.5, 0.109375, ((2, 4),))
    log_decay = draw_log_decay(jax.random.fold_in(jax.random.fold_in(seeds[4], part), 71), part)
    w_out = heavy_noise(seeds[3], (HEADS * HDIM, D), (HEADS * HDIM) ** -0.5, 0.125, ((0, 4),), (0, 1, 4, 2.0))
    return dict(tokens=tokens, w_qkv=w_qkv, log_decay=log_decay, w_out=w_out)


exact_mode = lax.Precision.HIGHEST

def rounded(array):
    return lax.optimization_barrier(array.astype(jnp.bfloat16)).astype(jnp.float32)

def local_blocks(queries, keys, value_rows, decays, block_rows):
    head_count, row_count, head_dim = queries.shape
    number_of_tiles = row_count // block_rows

    def blocked(array):
        return array.reshape(head_count, number_of_tiles, block_rows, head_dim).transpose(1, 0, 2, 3)
    attenuation_tiles = decays.reshape(head_count, number_of_tiles, block_rows).transpose(1, 0, 2)
    causal = jnp.arange(block_rows)[:, None] >= jnp.arange(block_rows)[None, :]

    def advance(memory, block):
        query_part, key_part, value_part, decay_part = block
        running = jnp.cumsum(decay_part, axis=1)
        spread = jnp.where(causal, running[:, :, None] - running[:, None, :], 0.0)
        weight = jnp.where(causal, jnp.exp(spread), 0.0)
        scores = jnp.einsum('htd,hsd->hts', query_part, key_part, precision=exact_mode)
        weighted = rounded(scores * weight)
        result = jnp.einsum('hts,hsd->htd', weighted, value_part, precision=exact_mode)
        query_scaled = rounded(query_part * jnp.exp(running)[:, :, None])
        state_used = rounded(memory)
        result = result + jnp.einsum('htd,hde->hte', query_scaled, state_used, precision=exact_mode)
        final_log = running[:, -1]
        key_scaled = rounded(key_part * jnp.exp(final_log[:, None] - running)[:, :, None])
        block_kv = jnp.einsum('htd,hte->hde', key_scaled, value_part, precision=exact_mode)
        memory = jnp.exp(final_log)[:, None, None] * memory + block_kv
        return (memory, result)
    start = jnp.zeros((head_count, head_dim, head_dim), jnp.float32)
    _, results = lax.scan(advance, start, (blocked(queries), blocked(keys), blocked(value_rows), attenuation_tiles))
    return results.transpose(1, 0, 2, 3).reshape(head_count, row_count, head_dim)

def reference(tokens, w_qkv, log_decay, w_out):
    projected = jnp.dot(tokens, w_qkv.reshape(D, 3 * HEADS * HDIM), preferred_element_type=jnp.float32)
    activated = jax.nn.silu(projected).astype(jnp.bfloat16).reshape(TOKENS, 3, HEADS, HDIM)
    queries = activated[:, 0].transpose(1, 0, 2).astype(jnp.float32)
    keys = activated[:, 1].transpose(1, 0, 2).astype(jnp.float32)
    value_rows = activated[:, 2].transpose(1, 0, 2).astype(jnp.float32)
    attended = local_blocks(queries, keys, value_rows, log_decay, BLK)
    normed = attended / jnp.sqrt(lax.optimization_barrier(jnp.mean(attended * attended, axis=2, keepdims=True)) + 1e-06)
    attn = normed.astype(jnp.bfloat16).transpose(1, 0, 2).reshape(TOKENS, HEADS * HDIM)
    width = H_DEV * HDIM
    summed = jnp.zeros((TOKENS, D), jnp.float32)
    for group in range(N_TENSOR):
        partial_g = jnp.dot(attn[:, group * width:(group + 1) * width], w_out[group * width:(group + 1) * width], preferred_element_type=jnp.float32).astype(jnp.bfloat16)
        partial_g = lax.optimization_barrier(partial_g)
        summed = summed + partial_g.astype(jnp.float32)
    return summed.astype(jnp.bfloat16)
```

```python
import functools

import jax
import jax.numpy as jnp
from jax import lax
from jax.experimental import pallas as pl
from jax.experimental.pallas import tpu as pltpu
from jax.sharding import PartitionSpec as P

BF16 = jnp.bfloat16
F32 = jnp.float32
HD = 128
CHUNK = 256
MIB = 1024 * 1024


def dot(a, b):
    return jnp.dot(a, b, preferred_element_type=F32)


def silu(x):
    return x / (1.0 + jnp.exp(-x))


def cost(flops, nbytes, trans=0):
    return pl.CostEstimate(flops=int(flops), bytes_accessed=int(nbytes), transcendentals=int(trans))


def project_kernel(n_x, has_acc, slots_ref, *refs):
    xs, ws, rest = refs[:n_x], refs[n_x : 2 * n_x], refs[2 * n_x :]
    total = rest[0][0] if has_acc else None
    for x, w in zip(xs, ws):
        term = dot(x[...], w[0])
        total = term if total is None else total + term
    rest[-1][0] = total


def project(slots, xs, w, acc, tile=512):
    rows, depth = xs[0].shape
    parts, _, width = w.shape
    n = len(xs)
    per = width // tile
    in_specs = [pl.BlockSpec((rows, depth), lambda j, s: (0, 0)) for _ in xs]
    in_specs += [
        pl.BlockSpec((1, depth, tile), lambda j, s, i=i: (j // per, s[i], j % per)) for i in range(n)
    ]
    block = pl.BlockSpec((1, rows, tile), lambda j, s: (j // per, 0, j % per))
    args = list(xs) + [w] * n
    if acc is not None:
        in_specs.append(block)
        args.append(acc)
    return pl.pallas_call(
        functools.partial(project_kernel, n, acc is not None),
        grid_spec=pltpu.PrefetchScalarGridSpec(
            num_scalar_prefetch=1, grid=(parts * per,), in_specs=in_specs, out_specs=block
        ),
        out_shape=jax.ShapeDtypeStruct((parts, rows, width), F32),
        compiler_params=pltpu.CompilerParams(vmem_limit_bytes=20 * MIB),
        cost_estimate=cost(2 * n * rows * depth * parts * width, n * depth * parts * width * 2 + rows * parts * width * 8),
        name="project",
    )(slots, *args)


def key_value_kernel(slots, xt, xb, wk, wv, ak, av, ek, etail, k_out, v_out, s1_out, s_out):
    half = xt.shape[0]
    for r, x in ((0, xt), (half, xb)):
        sl = pl.ds(r, half)
        k_out[sl, :] = silu(ak[0, sl, :] + dot(x[...], wk[0])).astype(BF16)
        v_out[sl, :] = silu(av[0, sl, :] + dot(x[...], wv[0])).astype(BF16)
    heads = k_out.shape[1] // HD
    for h in range(heads):
        cols = pl.ds(h * HD, HD)
        sums = []
        for c in range(k_out.shape[0] // CHUNK):
            sl = pl.ds(c * CHUNK, CHUNK)
            ks = (k_out[sl, cols].astype(F32) * ek[0, sl, h : h + 1]).astype(BF16)
            sums.append(
                lax.dot_general(ks, v_out[sl, cols], (((0,), (0,)), ((), ())), preferred_element_type=F32)
            )
        s1_out[h] = sums[0]
        s_out[h] = (sums[0] * etail[0, 0:1, h : h + 1] + sums[1]).astype(BF16)


def key_value(slots, xt, xb, w, acc, ek, etail, tile=512):
    rows = acc.shape[1]
    half, depth = xt.shape
    width = w.shape[2]
    per = width // tile
    hp = tile // HD
    heads = width // HD
    ek = ek.reshape(per, hp, rows).transpose(0, 2, 1)
    etail = etail.reshape(per, 1, hp)
    x_spec = pl.BlockSpec((half, depth), lambda j, s: (0, 0))
    return pl.pallas_call(
        key_value_kernel,
        grid_spec=pltpu.PrefetchScalarGridSpec(
            num_scalar_prefetch=1,
            grid=(per,),
            in_specs=[
                x_spec,
                x_spec,
                pl.BlockSpec((1, depth, tile), lambda j, s: (1, s[0], j)),
                pl.BlockSpec((1, depth, tile), lambda j, s: (2, s[0], j)),
                pl.BlockSpec((1, rows, tile), lambda j, s: (1, 0, j)),
                pl.BlockSpec((1, rows, tile), lambda j, s: (2, 0, j)),
                pl.BlockSpec((1, rows, hp), lambda j, s: (j, 0, 0)),
                pl.BlockSpec((1, 1, hp), lambda j, s: (j, 0, 0)),
            ],
            out_specs=[
                pl.BlockSpec((rows, tile), lambda j, s: (0, j)),
                pl.BlockSpec((rows, tile), lambda j, s: (0, j)),
                pl.BlockSpec((hp, HD, HD), lambda j, s: (j, 0, 0)),
                pl.BlockSpec((hp, HD, HD), lambda j, s: (j, 0, 0)),
            ],
        ),
        out_shape=[
            jax.ShapeDtypeStruct((rows, width), BF16),
            jax.ShapeDtypeStruct((rows, width), BF16),
            jax.ShapeDtypeStruct((heads, HD, HD), F32),
            jax.ShapeDtypeStruct((heads, HD, HD), BF16),
        ],
        compiler_params=pltpu.CompilerParams(vmem_limit_bytes=28 * MIB),
        cost_estimate=cost(4 * rows * depth * width, 8 * rows * width + 4 * depth * width),
        name="key_value",
    )(slots, xt, xb, w, w, acc, acc, ek, etail)


def inner_kernel(slots, xt, xb, wq, aq, k, v, acol, arow, q_out, o_out):
    half = xt.shape[0]
    for r, x in ((0, xt), (half, xb)):
        sl = pl.ds(r, half)
        q_out[sl, :] = silu(aq[0, sl, :] + dot(x[...], wq[0])).astype(BF16)
    t = lax.broadcasted_iota(jnp.int32, (CHUNK, CHUNK), 0)
    s = lax.broadcasted_iota(jnp.int32, (CHUNK, CHUNK), 1)
    causal = s <= t
    for h in range(q_out.shape[1] // HD):
        cols = pl.ds(h * HD, HD)
        for c in range(q_out.shape[0] // CHUNK):
            sl = pl.ds(c * CHUNK, CHUNK)
            scores = lax.dot_general(
                q_out[sl, cols], k[sl, cols], (((1,), (1,)), ((), ())), preferred_element_type=F32
            )
            spread = acol[0, sl, h : h + 1] - arow[0, h : h + 1, sl]
            weighted = jnp.where(causal, scores * jnp.exp(jnp.minimum(spread, 0.0)), 0.0)
            o_out[sl, cols] = dot(weighted.astype(BF16), v[sl, cols])


def inner(slots, xt, xb, w, acc, k, v, a, tile=256):
    rows = acc.shape[1]
    half, depth = xt.shape
    width = w.shape[2]
    per = width // tile
    hp = tile // HD
    arow = a.reshape(per, hp, rows)
    acol = arow.transpose(0, 2, 1)
    x_spec = pl.BlockSpec((half, depth), lambda j, s: (0, 0))
    tile_spec = pl.BlockSpec((rows, tile), lambda j, s: (0, j))
    return pl.pallas_call(
        inner_kernel,
        grid_spec=pltpu.PrefetchScalarGridSpec(
            num_scalar_prefetch=1,
            grid=(per,),
            in_specs=[
                x_spec,
                x_spec,
                pl.BlockSpec((1, depth, tile), lambda j, s: (0, s[0], j)),
                pl.BlockSpec((1, rows, tile), lambda j, s: (0, 0, j)),
                tile_spec,
                tile_spec,
                pl.BlockSpec((1, rows, hp), lambda j, s: (j, 0, 0)),
                pl.BlockSpec((1, hp, rows), lambda j, s: (j, 0, 0)),
            ],
            out_specs=[tile_spec, tile_spec],
        ),
        out_shape=[
            jax.ShapeDtypeStruct((rows, width), BF16),
            jax.ShapeDtypeStruct((rows, width), F32),
        ],
        compiler_params=pltpu.CompilerParams(vmem_limit_bytes=20 * MIB),
        cost_estimate=cost(2 * rows * depth * width + 4 * rows * CHUNK * width, 14 * rows * width + 2 * depth * width),
        name="inner",
    )(slots, xt, xb, w, acc, k, v, acol, arow)


def attend_kernel(slots, q, o, state, s1, ea, eh, w, attn, top, bot):
    half = top.shape[0]

    @pl.when(pl.program_id(0) == 0)
    def _():
        for h in range(q.shape[1] // HD):
            cols = pl.ds(h * HD, HD)
            first = state[h]
            second = first * eh[0:1, h : h + 1] + s1[h]
            for c, held in ((0, first), (1, second)):
                sl = pl.ds(c * CHUNK, CHUNK)
                qs = (q[sl, cols].astype(F32) * ea[sl, h : h + 1]).astype(BF16)
                out = o[sl, cols] + dot(qs, held.astype(BF16))
                mean = jnp.mean(out * out, axis=1, keepdims=True)
                attn[sl, cols] = (out * lax.rsqrt(mean + 1e-6)).astype(BF16)

    top[...] = dot(attn[pl.ds(0, half), :], w[...]).astype(BF16)
    bot[...] = dot(attn[pl.ds(half, half), :], w[...]).astype(BF16)


def attend(slots, q, o, state, s1, ea, eh, w_out, slice_width, tile=256):
    rows, width = q.shape
    heads = width // HD
    per = slice_width // tile
    half = rows // 2
    whole = lambda *shape: pl.BlockSpec(shape, lambda j, s: (0,) * len(shape))
    return pl.pallas_call(
        attend_kernel,
        grid_spec=pltpu.PrefetchScalarGridSpec(
            num_scalar_prefetch=1,
            grid=(per,),
            in_specs=[
                whole(rows, width),
                whole(rows, width),
                whole(heads, HD, HD),
                whole(heads, HD, HD),
                whole(rows, heads),
                whole(1, heads),
                pl.BlockSpec((width, tile), lambda j, s: (0, s[0] * per + j)),
            ],
            out_specs=[
                whole(rows, width),
                pl.BlockSpec((half, tile), lambda j, s: (0, j)),
                pl.BlockSpec((half, tile), lambda j, s: (0, j)),
            ],
        ),
        out_shape=[
            jax.ShapeDtypeStruct((rows, width), BF16),
            jax.ShapeDtypeStruct((half, slice_width), BF16),
            jax.ShapeDtypeStruct((half, slice_width), BF16),
        ],
        compiler_params=pltpu.CompilerParams(vmem_limit_bytes=28 * MIB),
        cost_estimate=cost(2 * rows * width * (HD + slice_width), rows * width * 8 + width * slice_width * 2),
        name="attend",
    )(slots, q, o, state, s1, ea, eh, w_out)


def output_kernel(slots, attn, wp, wm, wo, p_top, p_bot, m_top, m_bot, own):
    half = p_top.shape[0]
    for w, halves in ((wp, (p_top, p_bot)), (wm, (m_top, m_bot))):
        for i, out in enumerate(halves):
            out[...] = dot(attn[pl.ds(i * half, half), :], w[...]).astype(BF16)
    own[...] = dot(attn[...], wo[...]).astype(BF16)


def output(slots, attn, w_out, slice_width, tile=256):
    rows, width = attn.shape
    per = slice_width // tile
    half = rows // 2
    w_spec = lambda i: pl.BlockSpec((width, tile), lambda j, s: (0, s[i] * per + j))
    half_spec = pl.BlockSpec((half, tile), lambda j, s: (0, j))
    return pl.pallas_call(
        output_kernel,
        grid_spec=pltpu.PrefetchScalarGridSpec(
            num_scalar_prefetch=1,
            grid=(per,),
            in_specs=[pl.BlockSpec((rows, width), lambda j, s: (0, 0)), w_spec(0), w_spec(1), w_spec(2)],
            out_specs=[half_spec] * 4 + [pl.BlockSpec((rows, tile), lambda j, s: (0, j))],
        ),
        out_shape=[jax.ShapeDtypeStruct((half, slice_width), BF16)] * 4
        + [jax.ShapeDtypeStruct((rows, slice_width), BF16)],
        compiler_params=pltpu.CompilerParams(vmem_limit_bytes=20 * MIB),
        cost_estimate=cost(6 * rows * width * slice_width, 6 * width * slice_width + 8 * rows * slice_width),
        name="output",
    )(slots, attn, w_out, w_out, w_out)


def finish_kernel(own, lt, lb, rt, rb, out):
    half = lt.shape[0]
    for i, (a, b) in enumerate(((lt, rt), (lb, rb))):
        sl = pl.ds(i * half, half)
        out[sl, :] = (own[sl, :].astype(F32) + a[...].astype(F32) + b[...].astype(F32)).astype(BF16)


def finish(own, lt, lb, rt, rb):
    return pl.pallas_call(
        finish_kernel,
        out_shape=jax.ShapeDtypeStruct(own.shape, BF16),
        compiler_params=pltpu.CompilerParams(vmem_limit_bytes=16 * MIB),
        cost_estimate=cost(own.size * 2, own.size * 8),
        name="finish",
    )(own, lt, lb, rt, rb)


def body(n_y, tokens, w_qkv, log_decay, w_out):
    rows, slice_width = tokens.shape
    heads = log_decay.shape[0]
    n_t = lax.axis_size("tensor")
    n_seq = lax.axis_size("seq")
    n_z = n_seq // n_y
    me = lax.axis_index("tensor")
    pos = lax.axis_index("seq")
    my_z, my_y = pos // n_y, pos % n_y
    half = rows // 2

    def along_x(x, shift):
        return lax.ppermute(x, "tensor", [(i, (i + shift) % n_t) for i in range(n_t)])

    def along_y(x, shift):
        return lax.ppermute(
            x, "seq", [(z * n_y + y, z * n_y + (y + shift) % n_y) for z in range(n_z) for y in range(n_y)]
        )

    def along_z(x, shift):
        return lax.ppermute(
            x, "seq", [(z * n_y + y, (z + shift) * n_y + y) for z in range(n_z - shift) for y in range(n_y)]
        )

    def slot(*shifts):
        return jnp.stack([(me + s) % n_t for s in shifts]).astype(jnp.int32)

    left = along_x(tokens, 1)
    right = along_x(tokens, -1)

    chunks = rows // CHUNK
    a = jnp.cumsum(log_decay.reshape(heads, chunks, CHUNK), axis=2)
    ends = a[:, :, -1]
    shard_log = jnp.sum(ends, axis=1)
    ek = jnp.exp(ends[:, :, None] - a).reshape(heads, rows)
    a = a.reshape(heads, rows)
    ea = jnp.exp(a).T
    etail = jnp.exp(ends[:, 1])
    ehead = jnp.exp(ends[:, 0]).reshape(1, heads)

    row_logs = [shard_log] + [along_y(shard_log, d) for d in range(1, n_y)]
    ys = [(my_y - d) % n_y for d in range(n_y)]
    after = [
        sum(jnp.where(ys[e] > ys[d], row_logs[e], 0.0) for e in range(n_y)) for d in range(n_y)
    ]
    between = [
        sum(jnp.where((ys[e] > ys[d]) & (ys[e] < my_y), row_logs[e], 0.0) for e in range(n_y))
        for d in range(n_y)
    ]
    before = sum(jnp.where(ys[e] < my_y, row_logs[e], 0.0) for e in range(n_y))
    to_row_end = [jnp.exp(x) for x in after]
    to_here = [jnp.where(ys[d] < my_y, jnp.exp(between[d]), 0.0) for d in range(n_y)]
    row_log = sum(row_logs)
    other_rows = [along_z(row_log, e) for e in range(1, n_z)]
    from_row = []
    gap = before
    for e in range(1, n_z):
        from_row.append(jnp.where(e <= my_z, jnp.exp(gap), 0.0))
        gap = gap + other_rows[e - 1]

    w = w_qkv.transpose(1, 0, 2)
    acc = project(slot(0), [tokens], w, None)

    opp_top = along_x(left[:half], 1)
    opp_bot = along_x(right[half:], -1)
    acc = project(slot(-1, 1), [left, right], w, acc)

    far = slot(2)
    k, v, s1, shard_kv = key_value(far, opp_top, opp_bot, w, acc, ek, etail)

    def scaled(weight, x):
        return weight[:, None, None] * x.astype(F32)

    row_kvs = [shard_kv] + [along_y(shard_kv, d) for d in range(1, n_y)]
    q, o = inner(far, opp_top, opp_bot, w, acc, k, v, a)
    row_kv = sum(scaled(to_row_end[d], row_kvs[d]) for d in range(n_y)).astype(BF16)
    state = sum(scaled(to_here[d], row_kvs[d]) for d in range(1, n_y))
    earlier = [along_z(row_kv, e) for e in range(1, n_z)]
    state = state + sum(scaled(from_row[e - 1], earlier[e - 1]) for e in range(1, n_z))

    attn, far_top, far_bot = attend(far, q, o, state, s1, ea, ehead, w_out, slice_width)
    relay_top = along_x(far_top, 1)
    relay_bot = along_x(far_bot, -1)
    p_top, p_bot, m_top, m_bot, own = output(slot(1, -1, 0), attn, w_out, slice_width)
    left_bot = along_x(p_bot, 1)
    right_top = along_x(m_top, -1)
    left_top = along_x(p_top + relay_top, 1)
    right_bot = along_x(m_bot + relay_bot, -1)
    return finish(own, left_top, left_bot, right_top, right_bot)


def solution(mesh):
    in_specs = (
        P(("dp", "seq"), "tensor"),
        P(None, None, "tensor"),
        P("tensor", ("dp", "seq")),
        P("tensor", None),
    )
    out_specs = P(("dp", "seq"), "tensor")
    n_seq = mesh.shape["seq"]
    n_y = 4 if n_seq % 4 == 0 else 1
    return jax.shard_map(
        functools.partial(body, n_y), mesh=mesh, in_specs=in_specs, out_specs=out_specs, check_vma=False
    )
```

```python
import functools

import jax
import jax.numpy as jnp
from jax import lax
from jax.experimental import pallas as pl
from jax.experimental.pallas import tpu as pltpu
from jax.sharding import PartitionSpec as P

BF16 = jnp.bfloat16
F32 = jnp.float32
HD = 128
TILE = 2 * HD
CHUNK = 256
LOG_ROWS = 16
MIB = 1024 * 1024

ANY = pl.BlockSpec(memory_space=pl.ANY)
HBM = pl.BlockSpec(memory_space=pltpu.HBM)


def dot(a, b):
    return jnp.dot(a, b, preferred_element_type=F32)


def exact_dot(a, b):
    return jnp.dot(a, b, preferred_element_type=F32, precision=lax.Precision.HIGHEST)


def silu(x):
    half = 0.5 * x
    return half + half * jnp.tanh(half)


def whole(x):
    return pl.BlockSpec(x.shape, lambda i: (0,) * len(x.shape))


def like(dtype, *shape):
    return jax.ShapeDtypeStruct(shape, dtype)


def call(kernel, name, args, outs, mib, flops, nbytes, scratch=(), big=(), big_outs=(), aliases=None, loose=()):
    args = [pltpu.with_memory_space_constraint(a, pltpu.HBM) if i in big else a for i, a in enumerate(args)]
    return pl.pallas_call(
        kernel,
        grid=(1,),
        in_specs=[HBM if i in big else ANY if i in loose else whole(a) for i, a in enumerate(args)],
        out_specs=[HBM if i in big_outs else whole(a) for i, a in enumerate(outs)],
        out_shape=[pltpu.HBM(a.shape, a.dtype) if i in big_outs else a for i, a in enumerate(outs)],
        scratch_shapes=list(scratch),
        input_output_aliases=aliases or {},
        compiler_params=pltpu.CompilerParams(vmem_limit_bytes=mib * MIB),
        cost_estimate=pl.CostEstimate(flops=int(flops), bytes_accessed=int(nbytes), transcendentals=0),
        name=name,
    )(*args)


class Copies:
    def __init__(self, sems):
        self.sems, self.used = sems, 0

    def start(self, src, dst):
        copy = pltpu.make_async_copy(src, dst, self.sems.at[self.used])
        self.used += 1
        copy.start()
        return copy


class Stages:
    def __init__(self, copies, groups, ahead=2):
        self.copies, self.groups, self.ahead = copies, groups, ahead
        self.running = []
        for _ in range(min(ahead, len(groups))):
            self.begin()

    def begin(self):
        if len(self.running) < len(self.groups):
            self.running.append([self.copies.start(*pair) for pair in self.groups[len(self.running)]])

    def take(self, i):
        for r in self.running[i]:
            r.wait()
        self.begin()


def tensor_at(shift):
    n = lax.axis_size("tensor")
    return lax.rem(lax.axis_index("tensor") + (shift + n), n)


def decay_kernel(ld, ldt, arow, acol, ek, ea, ends, shard):
    heads, rows = ld.shape
    r = lax.broadcasted_iota(jnp.int32, (CHUNK, CHUNK), 0)
    c = lax.broadcasted_iota(jnp.int32, (CHUNK, CHUNK), 1)
    lower = (c <= r).astype(F32)
    upper = (r <= c).astype(F32)
    total = jnp.zeros((1, heads), F32)
    for i in range(rows // CHUNK):
        sl = pl.ds(i * CHUNK, CHUNK)
        down = exact_dot(lower, ldt[sl, :])
        end = down[CHUNK - 1 : CHUNK, :]
        arow[:, sl] = exact_dot(ld[:, sl], upper)
        acol[sl, :] = down
        ek[sl, :] = jnp.exp(jnp.minimum(end - down, 0.0))
        ea[sl, :] = jnp.exp(jnp.minimum(down, 0.0))
        ends[i : i + 1, :] = jnp.exp(jnp.minimum(end, 0.0))
        total = total + end
    shard[...] = jnp.zeros_like(shard)
    shard[0:1, 0:heads] = jnp.minimum(total, 0.0)


def decays(log_decay):
    heads, rows = log_decay.shape
    outs = [like(F32, heads, rows)] + [like(F32, rows, heads)] * 3
    outs += [like(F32, rows // CHUNK, heads), like(F32, 1, HD)]
    return call(decay_kernel, "decays", (log_decay, log_decay.T), outs, 4, 0, 1e5)


def piece_rows(w, part, place, depth):
    shift, half = place
    row = pl.multiple_of((tensor_at(shift) * 2 + half) * depth, HD)
    return w.at[part, pl.ds(row, depth), :]


def near_kernel(parts, places, *refs):
    n = len(places)
    pieces, (w, total, x, wv, sems) = refs[:n], refs[n:]
    depth = pieces[0].shape[1]
    groups = []
    for p, part in enumerate(parts):
        for i in range(0, n, 2):
            groups.append(
                [
                    (piece_rows(w, part, places[m], depth), wv.at[p, pl.ds(m * depth, depth), :])
                    for m in (i, i + 1)
                ]
            )
    stages = Stages(Copies(sems), groups, 3)
    for m in range(n):
        x[:, m * depth : (m + 1) * depth] = pieces[m][...]
    for p in range(len(parts)):
        for i in range(n // 2):
            stages.take(p * (n // 2) + i)
            rows = pl.ds(2 * i * depth, 2 * depth)
            for j in range(total.shape[1]):
                term = dot(x[:, rows], wv[p, rows, pl.ds(j * TILE, TILE)])
                total[p, j] = total[p, j] + term if i else term


def near(parts, places, pieces, w):
    rows, depth = pieces[0].shape
    width = w.shape[2]
    n, n_parts = len(pieces), len(parts)
    return call(
        functools.partial(near_kernel, parts, places),
        "near",
        [*pieces, w],
        [like(F32, n_parts, width // TILE, rows, TILE)],
        36,
        2 * n * rows * depth * n_parts * width,
        n * depth * n_parts * width * 2 + rows * n_parts * width * 4,
        scratch=[
            pltpu.VMEM((rows, n * depth), BF16),
            pltpu.VMEM((n_parts, n * depth, width), BF16),
            pltpu.SemaphoreType.DMA((n_parts * n,)),
        ],
        big=(n,),
    )[0]


def log_rows(log):
    high = log.astype(BF16).astype(F32)
    middle = (log - high).astype(BF16).astype(F32)
    low = log - high - middle
    row = lax.broadcasted_iota(jnp.int32, (LOG_ROWS, HD), 0)
    rows = jnp.where(row == 0, high, jnp.where(row == 1, middle, low))
    return jnp.where(row < 3, rows, 0.0).astype(BF16)


def log_of(message):
    tail = message[pl.ds(message.shape[0] - LOG_ROWS, LOG_ROWS), :].astype(F32)
    return jnp.minimum(tail[0:1] + tail[1:2] + tail[2:3], 0.0)


def place_along_y(n_y, shift=0):
    return lax.rem(lax.axis_index("seq") + (shift + n_y), n_y)


def key_value_kernel(n_y, f0, f1, w, total, ek, ends, shard, k_out, v_out, s1_out, *refs):
    messages, (x, wv, scaled, sv, sems) = refs[:n_y], refs[n_y:]
    n_tiles, rows, _ = k_out.shape
    depth = f0.shape[1]
    row = pl.multiple_of(tensor_at(2) * 2 * depth, HD)
    groups = []
    for i in range(2):
        for j in range(0, n_tiles, 2):
            cols = pl.ds(j * TILE, 2 * TILE)
            groups.append([(w.at[i + 1, pl.ds(row, 2 * depth), cols], wv.at[i, :, cols])])
    stages = Stages(Copies(sems), groups, 3)
    for i, f in enumerate((f0, f1)):
        x[:, i * depth : (i + 1) * depth] = f[...]
    group = n_tiles * 2 // n_y
    for i, out in enumerate((k_out, v_out)):
        for j in range(n_tiles):
            if j % 2 == 0:
                stages.take((i * n_tiles + j) // 2)
            made = silu(total[i, j] + dot(x[...], wv[i, :, pl.ds(j * TILE, TILE)])).astype(BF16)
            out[j] = made
            if i == 0:
                for b in range(2):
                    key = made[:, b * HD : (b + 1) * HD].astype(F32)
                    scaled[j, :, pl.ds(b * HD, HD)] = (key * ek[:, 2 * j + b : 2 * j + b + 1]).astype(BF16)
                continue
            both = []
            for c in range(rows // CHUNK):
                sl = pl.ds(c * CHUNK, CHUNK)
                both.append(
                    lax.dot_general(
                        scaled[j, sl, :], out[j, sl, :], (((0,), (0,)), ((), ())), preferred_element_type=F32
                    )
                )
            for b in range(2):
                h = 2 * j + b
                one = slice(b * HD, (b + 1) * HD)
                sums = [m[one, one] for m in both]
                s1_out[pl.ds(h * HD, HD), :] = sums[0]
                sv[h // group, pl.ds(h % group * HD, HD), :] = (
                    sums[0] * ends[1:2, h : h + 1] + sums[1]
                ).astype(BF16)
    for p in range(n_y):
        log = shard[...] if p == 0 else pltpu.roll(shard[...], HD - p * group, 1)
        sv[p, pl.ds(group * HD, LOG_ROWS), :] = log_rows(log)
    for d in range(n_y):
        messages[d][...] = sv[place_along_y(n_y, d)]


def key_value(n_y, far, w, total, ek, ends, shard):
    _, n_tiles, rows, _ = total.shape
    width = w.shape[2]
    depth = far[0].shape[1]
    size = (width // n_y + LOG_ROWS, HD)
    tiles = like(BF16, n_tiles, rows, TILE)
    return call(
        functools.partial(key_value_kernel, n_y),
        "key_value",
        (*far, w, total, ek, ends, shard),
        [tiles, tiles, like(F32, width, HD)] + [like(BF16, *size)] * n_y,
        32,
        4 * rows * 2 * depth * width,
        8 * rows * width + 8 * depth * width,
        scratch=[
            pltpu.VMEM((rows, 2 * depth), BF16),
            pltpu.VMEM((2, 2 * depth, width), BF16),
            pltpu.VMEM((n_tiles, rows, TILE), BF16),
            pltpu.VMEM((n_y, *size), BF16),
            pltpu.SemaphoreType.DMA((n_tiles,)),
        ],
        big=(2,),
    )


def query_kernel(places, *refs):
    n = len(places)
    pieces, (w, total, q_out, x, wv, sems) = refs[:n], refs[n:]
    depth = pieces[0].shape[1]
    groups = [
        [(piece_rows(w, 0, places[m], depth), wv.at[pl.ds(m * depth, depth), :]) for m in (i, i + 1)]
        for i in range(0, n, 2)
    ]
    stages = Stages(Copies(sems), groups, n // 2)
    for m in range(n):
        x[:, m * depth : (m + 1) * depth] = pieces[m][...]
    for i in range(n // 2):
        stages.take(i)
    for j in range(q_out.shape[0]):
        q_out[j] = silu(total[0, j] + dot(x[...], wv[:, pl.ds(j * TILE, TILE)])).astype(BF16)


def query(places, pieces, w, total):
    _, n_tiles, rows, _ = total.shape
    width = w.shape[2]
    n = len(pieces)
    depth = pieces[0].shape[1]
    return call(
        functools.partial(query_kernel, places),
        "query",
        (*pieces, w, total),
        [like(BF16, n_tiles, rows, TILE)],
        24,
        2 * rows * n * depth * width,
        6 * rows * width + 2 * n * depth * width,
        scratch=[
            pltpu.VMEM((rows, n * depth), BF16),
            pltpu.VMEM((n * depth, width), BF16),
            pltpu.SemaphoreType.DMA((n,)),
        ],
        big=(n,),
    )[0]


def inner_kernel(q, k, v, acol, arow, ea, qs_out, o_out):
    n_tiles, rows, _ = q.shape
    t = lax.broadcasted_iota(jnp.int32, (CHUNK, CHUNK), 0)
    s = lax.broadcasted_iota(jnp.int32, (CHUNK, CHUNK), 1)
    causal = s <= t
    for j in range(n_tiles):
        for b in range(2):
            h = 2 * j + b
            one = pl.ds(b * HD, HD)
            for c in range(rows // CHUNK):
                sl = pl.ds(c * CHUNK, CHUNK)
                scores = lax.dot_general(
                    q[j, sl, one], k[j, sl, one], (((1,), (1,)), ((), ())), preferred_element_type=F32
                )
                spread = acol[sl, h : h + 1] - arow[h : h + 1, sl]
                weighted = jnp.where(causal, scores * jnp.exp(jnp.minimum(spread, 0.0)), 0.0)
                o_out[j, sl, one] = dot(weighted.astype(BF16), v[j, sl, one])
                qs_out[j, sl, one] = (q[j, sl, one].astype(F32) * ea[sl, h : h + 1]).astype(BF16)


def inner(q, k, v, acol, arow, ea):
    n_tiles, rows, _ = k.shape
    tiles = (n_tiles, rows, TILE)
    return call(
        inner_kernel,
        "inner",
        (q, k, v, acol, arow, ea),
        [like(BF16, *tiles), like(F32, *tiles)],
        24,
        4 * rows * CHUNK * n_tiles * TILE,
        14 * rows * n_tiles * TILE,
    )


def sum_logs(choose, logs):
    total = jnp.zeros_like(logs[0])
    for y, log in enumerate(logs):
        total = total + jnp.where(choose(y), log, 0.0)
    return total


def row_kernel(n_y, *refs):
    messages, out = refs[:n_y], refs[n_y + 1]
    at = [place_along_y(n_y, -d) for d in range(n_y)]
    logs = [log_of(m) for m in messages]
    weights = [jnp.exp(sum_logs(lambda e: at[e] > at[d], logs)) for d in range(n_y)]
    for h in range(out.shape[0] // HD):
        one = pl.ds(h * HD, HD)
        total = None
        for weight, m in zip(weights, messages):
            term = m[one, :].astype(F32) * weight[:, h : h + 1]
            total = term if total is None else total + term
        out[one, :] = total.astype(BF16)
    out[pl.ds(out.shape[0] - LOG_ROWS, LOG_ROWS), :] = log_rows(sum(logs[1:], logs[0]))


def row_sum(messages, after):
    size = messages[0].shape
    n = len(messages)
    return call(
        functools.partial(row_kernel, n),
        "row_sum",
        (*messages, after),
        [like(BF16, *size)],
        4,
        8 * size[0] * HD,
        16 * size[0] * HD,
        big=(n,),
    )[0]


def state_kernel(n_y, n_z, *refs):
    messages, earlier, outs = refs[:n_y], refs[n_y : n_y + n_z - 1], refs[n_y + n_z :]
    my_z = lax.axis_index("seq") // n_y
    at = [place_along_y(n_y, -d) for d in range(n_y)]
    logs = [log_of(m) for m in messages]
    gap = jnp.zeros_like(logs[0])
    from_rows = []
    for e in range(1, n_z):
        from_rows.append(jnp.where(e <= my_z, jnp.exp(gap), 0.0))
        gap = gap + log_of(earlier[e - 1])
    for d in range(n_y):
        there = place_along_y(n_y, d)
        start = jnp.exp(sum_logs(lambda e: at[e] < there, logs))
        weights = [
            jnp.where(at[s] < there, jnp.exp(sum_logs(lambda e: (at[e] > at[s]) & (at[e] < there), logs)), 0.0)
            for s in range(n_y)
        ]
        for h in range(outs[d].shape[0] // HD):
            one = pl.ds(h * HD, HD)
            state = jnp.zeros((HD, HD), F32)
            for weight, m in zip(from_rows, earlier):
                state = state + m[one, :].astype(F32) * (weight[:, h : h + 1] * start[:, h : h + 1])
            for weight, m in zip(weights, messages):
                state = state + m[one, :].astype(F32) * weight[:, h : h + 1]
            outs[d][one, :] = state.astype(BF16)


def states(messages, earlier, after):
    n_y, n_z = len(messages), len(earlier) + 1
    rows = messages[0].shape[0] - LOG_ROWS
    return call(
        functools.partial(state_kernel, n_y, n_z),
        "states",
        (*messages, *earlier, after),
        [like(BF16, rows, HD)] * n_y,
        4,
        64 * rows * HD,
        24 * rows * HD,
        big=(n_y + n_z - 1,),
    )


def out_weights(w, shift, slice_width):
    start = pl.multiple_of(tensor_at(shift) * slice_width, HD)
    return w.at[:, pl.ds(start, slice_width)]


def attend_kernel(n_y, qs, o, w, s1, ends, *refs):
    received, (attn, top, bot, wv, state, sem) = refs[:n_y], refs[n_y:]
    half, slice_width = top.shape
    n_tiles = qs.shape[0]
    fetch = pltpu.make_async_copy(out_weights(w, 2, slice_width), wv, sem)
    fetch.start()
    size = received[0].shape[0]
    for d in range(n_y):
        row = pl.multiple_of(place_along_y(n_y, -d) * size, HD)
        state[pl.ds(row, size), :] = received[d][...]
    for j in range(n_tiles):
        for b in range(2):
            h = 2 * j + b
            cols = pl.ds(h * HD, HD)
            one = pl.ds(b * HD, HD)
            first = state[cols, :]
            second = (first.astype(F32) * ends[0:1, h : h + 1] + s1[cols, :]).astype(BF16)
            for c, held in ((0, first), (1, second)):
                sl = pl.ds(c * CHUNK, CHUNK)
                out = o[j, sl, one] + dot(qs[j, sl, one], held)
                mean = jnp.mean(out * out, axis=1, keepdims=True)
                attn[sl, cols] = (out * lax.rsqrt(mean + 1e-6)).astype(BF16)
    fetch.wait()
    for j in range(slice_width // TILE):
        cols = pl.ds(j * TILE, TILE)
        out = dot(attn[...], wv[:, cols]).astype(BF16)
        top[:, cols] = out[:half]
        bot[:, cols] = out[half:]


def attend(n_y, qs, o, w_out, s1, ends, received, slice_width):
    n_tiles, rows, _ = qs.shape
    width = n_tiles * TILE
    half = rows // 2
    return call(
        functools.partial(attend_kernel, n_y),
        "attend",
        (qs, o, w_out, s1, ends, *received),
        [like(BF16, rows, width), like(BF16, half, slice_width), like(BF16, half, slice_width)],
        24,
        2 * rows * width * (HD + slice_width),
        rows * width * 8 + width * slice_width * 2,
        scratch=[
            pltpu.VMEM((width, slice_width), BF16),
            pltpu.VMEM((width, HD), BF16),
            pltpu.SemaphoreType.DMA,
        ],
        big=(2,),
    )


def output_kernel(attn, w, p_top, p_bot, m_top, m_bot, own, wv, sems):
    half, slice_width = p_top.shape
    copies = Copies(sems)
    fetches = [copies.start(out_weights(w, shift, slice_width), wv.at[i]) for i, shift in enumerate((1, -1, 0))]
    for i, outs in enumerate(((p_top, p_bot), (m_top, m_bot), (own,))):
        fetches[i].wait()
        for j in range(slice_width // TILE):
            cols = pl.ds(j * TILE, TILE)
            out = dot(attn[...], wv[i, :, cols]).astype(BF16)
            if len(outs) == 1:
                own[:, cols] = out
            else:
                outs[0][:, cols] = out[:half]
                outs[1][:, cols] = out[half:]


def output(attn, w_out, slice_width):
    rows, width = attn.shape
    half = rows // 2
    return call(
        output_kernel,
        "output",
        (attn, w_out),
        [like(BF16, half, slice_width)] * 4 + [like(BF16, rows, slice_width)],
        16,
        6 * rows * width * slice_width,
        6 * width * slice_width + 8 * rows * slice_width,
        scratch=[pltpu.VMEM((3, width, slice_width), BF16), pltpu.SemaphoreType.DMA((3,))],
        big=(1,),
    )


def finish_kernel(own, lt, lb, rt, rb, out):
    half = lt.shape[0]
    for i, (a, b) in enumerate(((lt, rt), (lb, rb))):
        sl = pl.ds(i * half, half)
        out[sl, :] = (own[sl, :].astype(F32) + a[...].astype(F32) + b[...].astype(F32)).astype(BF16)


def finish(*parts):
    own = parts[0]
    return call(finish_kernel, "finish", parts, [like(BF16, *own.shape)], 8, own.size * 2, own.size * 8)[0]


def body(n_y, tokens, w_qkv, log_decay, w_out):
    slice_width = tokens.shape[1]
    n_t = lax.axis_size("tensor")
    n_z = lax.axis_size("seq") // n_y

    def along_x(x, shift):
        return lax.ppermute(x, "tensor", [(i, (i + shift) % n_t) for i in range(n_t)])

    def along_y(x, shift):
        return lax.ppermute(
            x, "seq", [(z * n_y + y, z * n_y + (y + shift) % n_y) for z in range(n_z) for y in range(n_y)]
        )

    def along_z(x, shift):
        return lax.ppermute(
            x, "seq", [(z * n_y + y, (z + shift) % n_z * n_y + y) for z in range(n_z) for y in range(n_y)]
        )

    w = w_qkv.transpose(1, 0, 2)
    part = slice_width // 2
    t0, t1 = tokens[:, :part], tokens[:, part:]

    l0 = along_x(t0, 1)
    r1 = along_x(t1, -1)
    l1 = along_x(t1, 1)
    r0 = along_x(t0, -1)
    f0 = along_x(l0, 1)
    f1 = along_x(r1, -1)
    pieces = {(0, 0): t0, (0, 1): t1, (-1, 0): l0, (-1, 1): l1, (1, 0): r0, (1, 1): r1, (2, 0): f0, (2, 1): f1}

    def take(*places):
        return places, [pieces[p] for p in places], w

    arow, acol, ek, ea, ends, shard = decays(log_decay)
    q_total = near((0,), *take((0, 0), (0, 1), (-1, 0), (1, 1)))
    total = near((1, 2), *take((0, 0), (0, 1), (-1, 0), (1, 1), (-1, 1), (1, 0)))
    k, v, s1, *kvs = key_value(n_y, (f0, f1), w, total, ek, ends, shard)

    sums = [kvs[0]] + [along_y(kvs[d], d) for d in range(1, n_y)]
    q = query(*take((-1, 1), (1, 0), (2, 0), (2, 1)), q_total)
    row = row_sum(sums, q)
    earlier = [along_z(row, e) for e in range(1, n_z)]
    qs, o = inner(q, k, v, acol, arow, ea)
    starts = states(sums, earlier, qs)
    received = [starts[0]] + [along_y(starts[d], d) for d in range(1, n_y)]

    attn, far_top, far_bot = attend(n_y, qs, o, w_out, s1, ends, received, slice_width)
    relay_top = along_x(far_top, 1)
    relay_bot = along_x(far_bot, -1)
    p_top, p_bot, m_top, m_bot, own = output(attn, w_out, slice_width)
    left_bot = along_x(p_bot, 1)
    right_top = along_x(m_top, -1)
    left_top = along_x(p_top + relay_top, 1)
    right_bot = along_x(m_bot + relay_bot, -1)
    return finish(own, left_top, left_bot, right_top, right_bot)


def solution(mesh):
    in_specs = (
        P(("dp", "seq"), "tensor"),
        P(None, None, "tensor"),
        P("tensor", ("dp", "seq")),
        P("tensor", None),
    )
    out_specs = P(("dp", "seq"), "tensor")
    n_seq = mesh.shape["seq"]
    n_y = 4 if n_seq % 4 == 0 else 1
    return jax.shard_map(
        functools.partial(body, n_y), mesh=mesh, in_specs=in_specs, out_specs=out_specs, check_vma=False
    )
```

```python
import functools

import jax
import jax.numpy as jnp
from jax import lax
from jax.experimental import pallas as pl
from jax.experimental.pallas import tpu as pltpu
from jax.sharding import PartitionSpec as P

BF16 = jnp.bfloat16
F32 = jnp.float32
HD = 128
TILE = 2 * HD
CHUNK = 256
LOG_ROWS = 16
MIB = 1024 * 1024

ANY = pl.BlockSpec(memory_space=pl.ANY)
HBM = pl.BlockSpec(memory_space=pltpu.HBM)


def dot(a, b):
    return jnp.dot(a, b, preferred_element_type=F32)


def exact_dot(a, b):
    return jnp.dot(a, b, preferred_element_type=F32, precision=lax.Precision.HIGHEST)


def silu(x):
    half = 0.5 * x
    return half + half * jnp.tanh(half)


def whole(x):
    return pl.BlockSpec(x.shape, lambda i: (0,) * len(x.shape))


def like(dtype, *shape):
    return jax.ShapeDtypeStruct(shape, dtype)


def call(kernel, name, args, outs, mib, flops, nbytes, scratch=(), big=(), big_outs=(), aliases=None, loose=()):
    args = [pltpu.with_memory_space_constraint(a, pltpu.HBM) if i in big else a for i, a in enumerate(args)]
    return pl.pallas_call(
        kernel,
        grid=(1,),
        in_specs=[HBM if i in big else ANY if i in loose else whole(a) for i, a in enumerate(args)],
        out_specs=[HBM if i in big_outs else whole(a) for i, a in enumerate(outs)],
        out_shape=[pltpu.HBM(a.shape, a.dtype) if i in big_outs else a for i, a in enumerate(outs)],
        scratch_shapes=list(scratch),
        input_output_aliases=aliases or {},
        compiler_params=pltpu.CompilerParams(vmem_limit_bytes=mib * MIB),
        cost_estimate=pl.CostEstimate(flops=int(flops), bytes_accessed=int(nbytes), transcendentals=0),
        name=name,
    )(*args)


MARK = like(F32, 8, HD)


class Copies:
    def __init__(self, sems):
        self.sems, self.used = sems, 0

    def start(self, src, dst):
        copy = pltpu.make_async_copy(src, dst, self.sems.at[self.used])
        self.used += 1
        copy.start()
        return copy


class Stages:
    def __init__(self, copies, groups, ahead=2):
        self.copies, self.groups, self.ahead = copies, groups, ahead
        self.running = []
        for _ in range(min(ahead, len(groups))):
            self.begin()

    def begin(self):
        if len(self.running) < len(self.groups):
            self.running.append([self.copies.start(*pair) for pair in self.groups[len(self.running)]])

    def take(self, i):
        for r in self.running[i]:
            r.wait()
        self.begin()


def tensor_at(shift):
    n = lax.axis_size("tensor")
    return lax.rem(lax.axis_index("tensor") + (shift + n), n)


def decay_kernel(ld, ldt, arow, acol, ek, ea, ends, shard):
    heads, rows = ld.shape
    r = lax.broadcasted_iota(jnp.int32, (CHUNK, CHUNK), 0)
    c = lax.broadcasted_iota(jnp.int32, (CHUNK, CHUNK), 1)
    lower = (c <= r).astype(F32)
    upper = (r <= c).astype(F32)
    total = jnp.zeros((1, heads), F32)
    for i in range(rows // CHUNK):
        sl = pl.ds(i * CHUNK, CHUNK)
        down = exact_dot(lower, ldt[sl, :])
        end = down[CHUNK - 1 : CHUNK, :]
        arow[:, sl] = exact_dot(ld[:, sl], upper)
        acol[sl, :] = down
        ek[sl, :] = jnp.exp(jnp.minimum(end - down, 0.0))
        ea[sl, :] = jnp.exp(jnp.minimum(down, 0.0))
        ends[i : i + 1, :] = jnp.exp(jnp.minimum(end, 0.0))
        total = total + end
    shard[...] = jnp.zeros_like(shard)
    shard[0:1, 0:heads] = jnp.minimum(total, 0.0)


def decays(log_decay):
    heads, rows = log_decay.shape
    outs = [like(F32, heads, rows)] + [like(F32, rows, heads)] * 3
    outs += [like(F32, rows // CHUNK, heads), like(F32, 1, HD)]
    return call(decay_kernel, "decays", (log_decay, log_decay.T), outs, 4, 0, 1e5)


def piece_rows(w, part, place, depth):
    shift, half = place
    row = pl.multiple_of((tensor_at(shift) * 2 + half) * depth, HD)
    return w.at[part, pl.ds(row, depth), :]


def near_kernel(places, ahead, has_before, has_weights, a, b, w, *refs):
    refs = list(refs)
    before = refs.pop(0) if has_before else None
    held = refs.pop(0) if has_weights else None
    total = refs.pop(0)
    fetched = refs.pop(0) if ahead else None
    x, *wv, sems = refs
    depth = a.shape[1]
    parts = w.shape[0]
    copies = Copies(sems)

    def rows_of(part, two, to):
        return [(piece_rows(w, part, place, depth), to.at[part, pl.ds(m * depth, depth), :]) for m, place in enumerate(two)]

    groups = [] if has_weights else [rows_of(p, places, wv[0]) for p in range(parts)]
    if ahead:
        groups += [rows_of(p, ahead, fetched) for p in range(parts)]
    stages = Stages(copies, groups, 3)
    x[:, :depth] = a[...]
    x[:, depth:] = b[...]
    for p in range(parts):
        if not has_weights:
            stages.take(p)
        source = held if has_weights else wv[0]
        for j in range(total.shape[1]):
            term = dot(x[...], source[p, :, pl.ds(j * TILE, TILE)])
            total[p, j] = before[p, j] + term if has_before else term
    if ahead:
        for p in range(parts):
            stages.take(p if has_weights else parts + p)


def near(places, two, w, before=None, held=None, ahead=None):
    rows, depth = two[0].shape
    parts, _, width = w.shape
    outs = [like(F32, parts, width // TILE, rows, TILE)]
    block = (parts, 2 * depth, width)
    if ahead:
        outs.append(like(BF16, *block))
    return call(
        functools.partial(near_kernel, places, ahead, before is not None, held is not None),
        "near",
        [*two, w] + [m for m in (before, held) if m is not None],
        outs,
        16,
        4 * rows * depth * parts * width,
        4 * depth * parts * width + rows * parts * width * 4,
        scratch=[pltpu.VMEM((rows, 2 * depth), BF16)]
        + ([] if held is not None else [pltpu.VMEM(block, BF16)])
        + [pltpu.SemaphoreType.DMA((4 * parts,))],
        big=(2,),
    )


def log_rows(log):
    high = log.astype(BF16).astype(F32)
    middle = (log - high).astype(BF16).astype(F32)
    low = log - high - middle
    row = lax.broadcasted_iota(jnp.int32, (LOG_ROWS, HD), 0)
    rows = jnp.where(row == 0, high, jnp.where(row == 1, middle, low))
    return jnp.where(row < 3, rows, 0.0).astype(BF16)


def log_of(message):
    tail = message[pl.ds(message.shape[0] - LOG_ROWS, LOG_ROWS), :].astype(F32)
    return jnp.minimum(tail[0:1] + tail[1:2] + tail[2:3], 0.0)


def place_along_y(n_y, shift=0):
    return lax.rem(lax.axis_index("seq") + (shift + n_y), n_y)


def key_value_kernel(n_y, f0, f1, w, total, ek, ends, shard, k_out, v_out, s1_out, *refs):
    messages, (x, scaled, sv) = refs[:n_y], refs[n_y:]
    n_tiles, rows, _ = k_out.shape
    depth = f0.shape[1]
    for i, f in enumerate((f0, f1)):
        x[:, i * depth : (i + 1) * depth] = f[...]
    group = n_tiles * 2 // n_y
    for i, out in enumerate((k_out, v_out)):
        for j in range(n_tiles):
            made = silu(total[i + 1, j] + dot(x[...], w[i + 1, :, pl.ds(j * TILE, TILE)])).astype(BF16)
            out[j] = made
            if i == 0:
                for b in range(2):
                    key = made[:, b * HD : (b + 1) * HD].astype(F32)
                    scaled[j, :, pl.ds(b * HD, HD)] = (key * ek[:, 2 * j + b : 2 * j + b + 1]).astype(BF16)
                continue
            both = []
            for c in range(rows // CHUNK):
                sl = pl.ds(c * CHUNK, CHUNK)
                both.append(
                    lax.dot_general(
                        scaled[j, sl, :], out[j, sl, :], (((0,), (0,)), ((), ())), preferred_element_type=F32
                    )
                )
            for b in range(2):
                h = 2 * j + b
                one = slice(b * HD, (b + 1) * HD)
                sums = [m[one, one] for m in both]
                s1_out[pl.ds(h * HD, HD), :] = sums[0]
                sv[h // group, pl.ds(h % group * HD, HD), :] = (
                    sums[0] * ends[1:2, h : h + 1] + sums[1]
                ).astype(BF16)
    for p in range(n_y):
        log = shard[...] if p == 0 else pltpu.roll(shard[...], HD - p * group, 1)
        sv[p, pl.ds(group * HD, LOG_ROWS), :] = log_rows(log)
    for d in range(n_y):
        messages[d][...] = sv[place_along_y(n_y, d)]


def key_value(n_y, far, w, total, ek, ends, shard):
    _, n_tiles, rows, _ = total.shape
    width = w.shape[2]
    depth = far[0].shape[1]
    size = (width // n_y + LOG_ROWS, HD)
    tiles = like(BF16, n_tiles, rows, TILE)
    return call(
        functools.partial(key_value_kernel, n_y),
        "key_value",
        (*far, w, total, ek, ends, shard),
        [tiles, tiles, like(F32, width, HD)] + [like(BF16, *size)] * n_y,
        16,
        4 * rows * 2 * depth * width,
        8 * rows * width + 8 * depth * width,
        scratch=[
            pltpu.VMEM((rows, 2 * depth), BF16),
            pltpu.VMEM((n_tiles, rows, TILE), BF16),
            pltpu.VMEM((n_y, *size), BF16),
        ],
    )


def query_kernel(f0, f1, w, total, q_out, x):
    depth = f0.shape[1]
    for i, f in enumerate((f0, f1)):
        x[:, i * depth : (i + 1) * depth] = f[...]
    for j in range(q_out.shape[0]):
        q_out[j] = silu(total[0, j] + dot(x[...], w[0, :, pl.ds(j * TILE, TILE)])).astype(BF16)


def query(far, w, total):
    _, n_tiles, rows, _ = total.shape
    depth = 2 * far[0].shape[1]
    return call(
        query_kernel,
        "query",
        (*far, w, total),
        [like(BF16, n_tiles, rows, TILE)],
        12,
        2 * rows * depth * n_tiles * TILE,
        6 * rows * n_tiles * TILE,
        scratch=[pltpu.VMEM((rows, depth), BF16)],
    )[0]


def inner_kernel(q, k, v, acol, arow, ea, qs_out, o_out, mark):
    mark[...] = jnp.zeros_like(mark)
    n_tiles, rows, _ = q.shape
    t = lax.broadcasted_iota(jnp.int32, (CHUNK, CHUNK), 0)
    s = lax.broadcasted_iota(jnp.int32, (CHUNK, CHUNK), 1)
    causal = s <= t
    for j in range(n_tiles):
        for b in range(2):
            h = 2 * j + b
            one = pl.ds(b * HD, HD)
            for c in range(rows // CHUNK):
                sl = pl.ds(c * CHUNK, CHUNK)
                scores = lax.dot_general(
                    q[j, sl, one], k[j, sl, one], (((1,), (1,)), ((), ())), preferred_element_type=F32
                )
                spread = acol[sl, h : h + 1] - arow[h : h + 1, sl]
                weighted = jnp.where(causal, scores * jnp.exp(jnp.minimum(spread, 0.0)), 0.0)
                o_out[j, sl, one] = dot(weighted.astype(BF16), v[j, sl, one])
                qs_out[j, sl, one] = (q[j, sl, one].astype(F32) * ea[sl, h : h + 1]).astype(BF16)


def inner(q, k, v, acol, arow, ea):
    n_tiles, rows, _ = k.shape
    tiles = (n_tiles, rows, TILE)
    return call(
        inner_kernel,
        "inner",
        (q, k, v, acol, arow, ea),
        [like(BF16, *tiles), like(F32, *tiles), MARK],
        16,
        4 * rows * CHUNK * n_tiles * TILE,
        14 * rows * n_tiles * TILE,
    )


def sum_logs(choose, logs):
    total = jnp.zeros_like(logs[0])
    for y, log in enumerate(logs):
        total = total + jnp.where(choose(y), log, 0.0)
    return total


def row_kernel(n_y, *refs):
    messages, (mark, out, done) = refs[:n_y], refs[n_y:]
    done[...] = mark[...]
    at = [place_along_y(n_y, -d) for d in range(n_y)]
    logs = [log_of(m) for m in messages]
    weights = [jnp.exp(sum_logs(lambda e: at[e] > at[d], logs)) for d in range(n_y)]
    for h in range(out.shape[0] // HD):
        one = pl.ds(h * HD, HD)
        total = None
        for weight, m in zip(weights, messages):
            term = m[one, :].astype(F32) * weight[:, h : h + 1]
            total = term if total is None else total + term
        out[one, :] = total.astype(BF16)
    out[pl.ds(out.shape[0] - LOG_ROWS, LOG_ROWS), :] = log_rows(sum(logs[1:], logs[0]))


def row_sum(messages, after):
    size = messages[0].shape
    n = len(messages)
    return call(
        functools.partial(row_kernel, n),
        "row_sum",
        (*messages, after),
        [like(BF16, *size), MARK],
        4,
        8 * size[0] * HD,
        16 * size[0] * HD,
    )


def state_kernel(n_y, n_z, *refs):
    messages, earlier, outs = refs[:n_y], refs[n_y : n_y + n_z - 1], refs[n_y + n_z :]
    my_z = lax.axis_index("seq") // n_y
    at = [place_along_y(n_y, -d) for d in range(n_y)]
    logs = [log_of(m) for m in messages]
    gap = jnp.zeros_like(logs[0])
    from_rows = []
    for e in range(1, n_z):
        from_rows.append(jnp.where(e <= my_z, jnp.exp(gap), 0.0))
        gap = gap + log_of(earlier[e - 1])
    for d in range(n_y):
        there = place_along_y(n_y, d)
        start = jnp.exp(sum_logs(lambda e: at[e] < there, logs))
        weights = [
            jnp.where(at[s] < there, jnp.exp(sum_logs(lambda e: (at[e] > at[s]) & (at[e] < there), logs)), 0.0)
            for s in range(n_y)
        ]
        for h in range(outs[d].shape[0] // HD):
            one = pl.ds(h * HD, HD)
            state = jnp.zeros((HD, HD), F32)
            for weight, m in zip(from_rows, earlier):
                state = state + m[one, :].astype(F32) * (weight[:, h : h + 1] * start[:, h : h + 1])
            for weight, m in zip(weights, messages):
                state = state + m[one, :].astype(F32) * weight[:, h : h + 1]
            outs[d][one, :] = state.astype(BF16)


def states(messages, earlier, after):
    n_y, n_z = len(messages), len(earlier) + 1
    rows = messages[0].shape[0] - LOG_ROWS
    return call(
        functools.partial(state_kernel, n_y, n_z),
        "states",
        (*messages, *earlier, after),
        [like(BF16, rows, HD)] * n_y,
        4,
        64 * rows * HD,
        24 * rows * HD,
    )


def fetch_kernel(shifts, w, mark, out, done, sems):
    copies = Copies(sems)
    slice_width = out.shape[2]
    reads = []
    for i, shift in enumerate(shifts):
        start = pl.multiple_of(tensor_at(shift) * slice_width, HD)
        reads.append(copies.start(w.at[:, pl.ds(start, slice_width)], out.at[i]))
    done[...] = mark[...]
    for r in reads:
        r.wait()


def fetch_out(shifts, w_out, slice_width, after):
    n = len(shifts)
    return call(
        functools.partial(fetch_kernel, shifts),
        "fetch_out",
        (w_out, after),
        [like(BF16, n, w_out.shape[0], slice_width), MARK],
        4,
        0,
        2 * w_out.size,
        scratch=[pltpu.SemaphoreType.DMA((n,))],
        big=(0,),
    )


def attend_kernel(n_y, qs, o, w, s1, ends, *refs):
    received, (attn, top, bot, state) = refs[:n_y], refs[n_y:]
    half, slice_width = top.shape
    n_tiles = qs.shape[0]
    size = received[0].shape[0]
    for d in range(n_y):
        row = pl.multiple_of(place_along_y(n_y, -d) * size, HD)
        state[pl.ds(row, size), :] = received[d][...]
    for j in range(n_tiles):
        for b in range(2):
            h = 2 * j + b
            cols = pl.ds(h * HD, HD)
            one = pl.ds(b * HD, HD)
            first = state[cols, :]
            second = (first.astype(F32) * ends[0:1, h : h + 1] + s1[cols, :]).astype(BF16)
            for c, held in ((0, first), (1, second)):
                sl = pl.ds(c * CHUNK, CHUNK)
                out = o[j, sl, one] + dot(qs[j, sl, one], held)
                mean = jnp.mean(out * out, axis=1, keepdims=True)
                attn[sl, cols] = (out * lax.rsqrt(mean + 1e-6)).astype(BF16)
    for j in range(slice_width // TILE):
        cols = pl.ds(j * TILE, TILE)
        out = dot(attn[...], w[0, :, cols]).astype(BF16)
        top[:, cols] = out[:half]
        bot[:, cols] = out[half:]


def attend(n_y, qs, o, w_out, s1, ends, received, slice_width):
    n_tiles, rows, _ = qs.shape
    width = n_tiles * TILE
    half = rows // 2
    return call(
        functools.partial(attend_kernel, n_y),
        "attend",
        (qs, o, w_out, s1, ends, *received),
        [like(BF16, rows, width), like(BF16, half, slice_width), like(BF16, half, slice_width)],
        16,
        2 * rows * width * (HD + slice_width),
        rows * width * 8 + width * slice_width * 2,
        scratch=[pltpu.VMEM((width, HD), BF16)],
    )


def output_kernel(attn, w, p_top, p_bot, m_top, m_bot, own):
    half, slice_width = p_top.shape
    for i, outs in enumerate(((p_top, p_bot), (m_top, m_bot), (own,))):
        for j in range(slice_width // TILE):
            cols = pl.ds(j * TILE, TILE)
            out = dot(attn[...], w[i + 1, :, cols]).astype(BF16)
            if len(outs) == 1:
                own[:, cols] = out
            else:
                outs[0][:, cols] = out[:half]
                outs[1][:, cols] = out[half:]


def output(attn, w_out, slice_width):
    rows, width = attn.shape
    half = rows // 2
    return call(
        output_kernel,
        "output",
        (attn, w_out),
        [like(BF16, half, slice_width)] * 4 + [like(BF16, rows, slice_width)],
        16,
        6 * rows * width * slice_width,
        6 * width * slice_width + 8 * rows * slice_width,
    )


def finish_kernel(own, lt, lb, rt, rb, out):
    half = lt.shape[0]
    for i, (a, b) in enumerate(((lt, rt), (lb, rb))):
        sl = pl.ds(i * half, half)
        out[sl, :] = (own[sl, :].astype(F32) + a[...].astype(F32) + b[...].astype(F32)).astype(BF16)


def finish(*parts):
    own = parts[0]
    return call(finish_kernel, "finish", parts, [like(BF16, *own.shape)], 8, own.size * 2, own.size * 8)[0]


def body(n_y, tokens, w_qkv, log_decay, w_out):
    slice_width = tokens.shape[1]
    n_t = lax.axis_size("tensor")
    n_z = lax.axis_size("seq") // n_y

    def along_x(x, shift):
        return lax.ppermute(x, "tensor", [(i, (i + shift) % n_t) for i in range(n_t)])

    def along_y(x, shift):
        return lax.ppermute(
            x, "seq", [(z * n_y + y, z * n_y + (y + shift) % n_y) for z in range(n_z) for y in range(n_y)]
        )

    def along_z(x, shift):
        return lax.ppermute(
            x, "seq", [(z * n_y + y, (z + shift) % n_z * n_y + y) for z in range(n_z) for y in range(n_y)]
        )

    w = w_qkv.transpose(1, 0, 2)
    part = slice_width // 2
    t0, t1 = tokens[:, :part], tokens[:, part:]

    l0 = along_x(t0, 1)
    r1 = along_x(t1, -1)
    l1 = along_x(t1, 1)
    r0 = along_x(t0, -1)
    f0 = along_x(l0, 1)
    f1 = along_x(r1, -1)

    arow, acol, ek, ea, ends, shard = decays(log_decay)
    far_places = ((2, 0), (2, 1))
    side_places = ((-1, 1), (1, 0))
    total = near(((0, 0), (0, 1)), (t0, t1), w)[0]
    total, w_side = near(((-1, 0), (1, 1)), (l0, r1), w, total, ahead=side_places)
    total, w_far = near(side_places, (l1, r0), w, total, w_side, ahead=far_places)
    far = (f0, f1)
    k, v, s1, *kvs = key_value(n_y, far, w_far, total, ek, ends, shard)

    sums = [kvs[0]] + [along_y(kvs[d], d) for d in range(1, n_y)]
    q = query(far, w_far, total)
    qs, o, mark = inner(q, k, v, acol, arow, ea)
    row, mark = row_sum(sums, mark)
    earlier = [along_z(row, e) for e in range(1, n_z)]
    w_slices, mark = fetch_out((2, 1, -1, 0), w_out, slice_width, mark)
    starts = states(sums, earlier, mark)
    received = [starts[0]] + [along_y(starts[d], d) for d in range(1, n_y)]

    attn, far_top, far_bot = attend(n_y, qs, o, w_slices, s1, ends, received, slice_width)
    relay_top = along_x(far_top, 1)
    relay_bot = along_x(far_bot, -1)
    p_top, p_bot, m_top, m_bot, own = output(attn, w_slices, slice_width)
    left_bot = along_x(p_bot, 1)
    right_top = along_x(m_top, -1)
    left_top = along_x(p_top + relay_top, 1)
    right_bot = along_x(m_bot + relay_bot, -1)
    return finish(own, left_top, left_bot, right_top, right_bot)


def solution(mesh):
    in_specs = (
        P(("dp", "seq"), "tensor"),
        P(None, None, "tensor"),
        P("tensor", ("dp", "seq")),
        P("tensor", None),
    )
    out_specs = P(("dp", "seq"), "tensor")
    n_seq = mesh.shape["seq"]
    n_y = 4 if n_seq % 4 == 0 else 1
    return jax.shard_map(
        functools.partial(body, n_y), mesh=mesh, in_specs=in_specs, out_specs=out_specs, check_vma=False
    )
```

```python
import functools

import jax
import jax.numpy as jnp
from jax import lax
from jax.experimental import pallas as pl
from jax.experimental.pallas import tpu as pltpu
from jax.sharding import PartitionSpec as P

BF16 = jnp.bfloat16
F32 = jnp.float32
HD = 128
TILE = 2 * HD
CHUNK = 256
LOG_ROWS = 16
MIB = 1024 * 1024

ANY = pl.BlockSpec(memory_space=pl.ANY)
HBM = pl.BlockSpec(memory_space=pltpu.HBM)


def dot(a, b):
    return jnp.dot(a, b, preferred_element_type=F32)


def exact_dot(a, b):
    return jnp.dot(a, b, preferred_element_type=F32, precision=lax.Precision.HIGHEST)


def silu(x):
    half = 0.5 * x
    return half + half * jnp.tanh(half)


def whole(x):
    return pl.BlockSpec(x.shape, lambda i: (0,) * len(x.shape))


def like(dtype, *shape):
    return jax.ShapeDtypeStruct(shape, dtype)


def call(kernel, name, args, outs, mib, flops, nbytes, scratch=(), big=(), big_outs=(), aliases=None, loose=()):
    args = [pltpu.with_memory_space_constraint(a, pltpu.HBM) if i in big else a for i, a in enumerate(args)]
    return pl.pallas_call(
        kernel,
        grid=(1,),
        in_specs=[HBM if i in big else ANY if i in loose else whole(a) for i, a in enumerate(args)],
        out_specs=[HBM if i in big_outs else whole(a) for i, a in enumerate(outs)],
        out_shape=[pltpu.HBM(a.shape, a.dtype) if i in big_outs else a for i, a in enumerate(outs)],
        scratch_shapes=list(scratch),
        input_output_aliases=aliases or {},
        compiler_params=pltpu.CompilerParams(vmem_limit_bytes=mib * MIB),
        cost_estimate=pl.CostEstimate(flops=int(flops), bytes_accessed=int(nbytes), transcendentals=0),
        name=name,
    )(*args)


MARK = like(F32, 8, HD)


class Copies:
    def __init__(self, sems):
        self.sems, self.used = sems, 0

    def start(self, src, dst):
        copy = pltpu.make_async_copy(src, dst, self.sems.at[self.used])
        self.used += 1
        copy.start()
        return copy


class Stages:
    def __init__(self, copies, groups, ahead=2):
        self.copies, self.groups, self.ahead = copies, groups, ahead
        self.running = []
        for _ in range(min(ahead, len(groups))):
            self.begin()

    def begin(self):
        if len(self.running) < len(self.groups):
            self.running.append([self.copies.start(*pair) for pair in self.groups[len(self.running)]])

    def take(self, i):
        for r in self.running[i]:
            r.wait()
        self.begin()


def tensor_at(shift):
    n = lax.axis_size("tensor")
    return lax.rem(lax.axis_index("tensor") + (shift + n), n)


def decay_kernel(ld, ldt, arow, acol, ek, ea, ends, shard):
    heads, rows = ld.shape
    r = lax.broadcasted_iota(jnp.int32, (CHUNK, CHUNK), 0)
    c = lax.broadcasted_iota(jnp.int32, (CHUNK, CHUNK), 1)
    lower = (c <= r).astype(F32)
    upper = (r <= c).astype(F32)
    total = jnp.zeros((1, heads), F32)
    for i in range(rows // CHUNK):
        sl = pl.ds(i * CHUNK, CHUNK)
        down = exact_dot(lower, ldt[sl, :])
        end = down[CHUNK - 1 : CHUNK, :]
        arow[:, sl] = exact_dot(ld[:, sl], upper)
        acol[sl, :] = down
        ek[sl, :] = jnp.exp(jnp.minimum(end - down, 0.0))
        ea[sl, :] = jnp.exp(jnp.minimum(down, 0.0))
        ends[i : i + 1, :] = jnp.exp(jnp.minimum(end, 0.0))
        total = total + end
    shard[...] = jnp.zeros_like(shard)
    shard[0:1, 0:heads] = jnp.minimum(total, 0.0)


def decays(log_decay):
    heads, rows = log_decay.shape
    outs = [like(F32, heads, rows)] + [like(F32, rows, heads)] * 3
    outs += [like(F32, rows // CHUNK, heads), like(F32, 1, HD)]
    return call(decay_kernel, "decays", (log_decay, log_decay.T), outs, 4, 0, 1e5)


def piece_rows(w, part, place, depth):
    shift, half = place
    row = pl.multiple_of((tensor_at(shift) * 2 + half) * depth, HD)
    return w.at[part, pl.ds(row, depth), :]


def near_kernel(places, ahead, has_before, has_weights, a, b, w, *refs):
    refs = list(refs)
    before = refs.pop(0) if has_before else None
    held = refs.pop(0) if has_weights else None
    total = refs.pop(0)
    fetched = refs.pop(0) if ahead else None
    x, *wv, sems = refs
    depth = a.shape[1]
    parts = w.shape[0]
    copies = Copies(sems)

    def rows_of(part, two, to):
        return [(piece_rows(w, part, place, depth), to.at[part, pl.ds(m * depth, depth), :]) for m, place in enumerate(two)]

    groups = [] if has_weights else [rows_of(p, places, wv[0]) for p in range(parts)]
    if ahead:
        groups += [rows_of(p, ahead, fetched) for p in range(parts)]
    stages = Stages(copies, groups, 3)
    x[:, :depth] = a[...]
    x[:, depth:] = b[...]
    for p in range(parts):
        if not has_weights:
            stages.take(p)
        source = held if has_weights else wv[0]
        for j in range(total.shape[1]):
            term = dot(x[...], source[p, :, pl.ds(j * TILE, TILE)])
            total[p, j] = before[p, j] + term if has_before else term
    if ahead:
        for p in range(parts):
            stages.take(p if has_weights else parts + p)


def near(places, two, w, before=None, held=None, ahead=None):
    rows, depth = two[0].shape
    parts, _, width = w.shape
    outs = [like(F32, parts, width // TILE, rows, TILE)]
    block = (parts, 2 * depth, width)
    if ahead:
        outs.append(like(BF16, *block))
    return call(
        functools.partial(near_kernel, places, ahead, before is not None, held is not None),
        "near",
        [*two, w] + [m for m in (before, held) if m is not None],
        outs,
        16,
        4 * rows * depth * parts * width,
        4 * depth * parts * width + rows * parts * width * 4,
        scratch=[pltpu.VMEM((rows, 2 * depth), BF16)]
        + ([] if held is not None else [pltpu.VMEM(block, BF16)])
        + [pltpu.SemaphoreType.DMA((4 * parts,))],
        big=(2,),
    )


def split_kernel(tokens, w, t0, t1, early, x, wv, tv, sems):
    depth = t0.shape[1]
    parts = w.shape[0]
    copies = Copies(sems)
    reads = [copies.start(tokens.at[:, pl.ds(m * depth, depth)], t) for m, t in enumerate((t0, t1))]
    first = lax.axis_index("dp") == 0
    later = Copies(sems.at[pl.ds(2, parts + parts * tv.shape[1])])

    @pl.when(first)
    def _():
        row = pl.multiple_of(tensor_at(0) * 2 * depth, HD)
        fetches = [later.start(w.at[p, pl.ds(row, 2 * depth), :], wv.at[p]) for p in range(parts)]
        for r in reads:
            r.wait()
        x[:, :depth] = t0[...]
        x[:, depth:] = t1[...]
        writes = []
        for p in range(parts):
            fetches[p].wait()
            for j in range(tv.shape[1]):
                tv[p, j] = dot(x[...], wv[p, :, pl.ds(j * TILE, TILE)])
                writes.append(later.start(tv.at[p, j], early.at[p, j]))
        for r in writes:
            r.wait()

    @pl.when(jnp.logical_not(first))
    def _():
        for r in reads:
            r.wait()


def split(tokens, w):
    rows, width = tokens.shape
    parts, _, columns = w.shape
    block = (parts, columns // TILE, rows, TILE)
    return call(
        split_kernel,
        "split",
        (tokens, w),
        [like(BF16, rows, width // 2)] * 2 + [like(F32, *block)],
        16,
        2 * rows * width * parts * columns,
        2 * width * parts * columns,
        scratch=[
            pltpu.VMEM((rows, width), BF16),
            pltpu.VMEM((parts, width, columns), BF16),
            pltpu.VMEM(block, F32),
            pltpu.SemaphoreType.DMA((2 + parts + parts * block[1],)),
        ],
        big=range(2),
        big_outs=(2,),
    )


def own_kernel(t0, t1, w, early, total, x, wv, sems):
    depth = t0.shape[1]
    parts = w.shape[0]
    copies = Copies(sems)
    first = lax.axis_index("dp") == 0

    @pl.when(first)
    def _():
        copy = copies.start(early, total)
        copy.wait()

    @pl.when(jnp.logical_not(first))
    def _():
        row = pl.multiple_of(tensor_at(0) * 2 * depth, HD)
        fetches = [copies.start(w.at[p, pl.ds(row, 2 * depth), :], wv.at[p]) for p in range(parts)]
        x[:, :depth] = t0[...]
        x[:, depth:] = t1[...]
        for p in range(parts):
            fetches[p].wait()
            for j in range(total.shape[1]):
                total[p, j] = dot(x[...], wv[p, :, pl.ds(j * TILE, TILE)])


def own_products(t0, t1, w, early):
    rows, depth = t0.shape
    parts, _, columns = w.shape
    return call(
        own_kernel,
        "own",
        (t0, t1, w, early),
        [like(F32, *early.shape)],
        16,
        4 * rows * depth * parts * columns,
        4 * depth * parts * columns,
        scratch=[
            pltpu.VMEM((rows, 2 * depth), BF16),
            pltpu.VMEM((parts, 2 * depth, columns), BF16),
            pltpu.SemaphoreType.DMA((parts + 1,)),
        ],
        big=(2, 3),
    )[0]


def log_rows(log):
    high = log.astype(BF16).astype(F32)
    middle = (log - high).astype(BF16).astype(F32)
    low = log - high - middle
    row = lax.broadcasted_iota(jnp.int32, (LOG_ROWS, HD), 0)
    rows = jnp.where(row == 0, high, jnp.where(row == 1, middle, low))
    return jnp.where(row < 3, rows, 0.0).astype(BF16)


def log_of(message):
    tail = message[pl.ds(message.shape[0] - LOG_ROWS, LOG_ROWS), :].astype(F32)
    return jnp.minimum(tail[0:1] + tail[1:2] + tail[2:3], 0.0)


def send_order(n):
    return range(n - 1, 0, -1)


def place_along_y(n_y, shift=0):
    return lax.rem(lax.axis_index("seq") + (shift + n_y), n_y)


def key_value_kernel(n_y, f0, f1, w, total, ek, ends, shard, mark, k_out, v_out, s1_out, *refs):
    messages, (x, scaled, sv) = refs[:n_y], refs[n_y:]
    n_tiles, rows, _ = k_out.shape
    depth = f0.shape[1]
    for i, f in enumerate((f0, f1)):
        x[:, i * depth : (i + 1) * depth] = f[...]
    group = n_tiles * 2 // n_y
    for i, out in enumerate((k_out, v_out)):
        for j in range(n_tiles):
            made = silu(total[i + 1, j] + dot(x[...], w[i + 1, :, pl.ds(j * TILE, TILE)])).astype(BF16)
            out[j] = made
            if i == 0:
                for b in range(2):
                    key = made[:, b * HD : (b + 1) * HD].astype(F32)
                    scaled[j, :, pl.ds(b * HD, HD)] = (key * ek[:, 2 * j + b : 2 * j + b + 1]).astype(BF16)
                continue
            both = []
            for c in range(rows // CHUNK):
                sl = pl.ds(c * CHUNK, CHUNK)
                both.append(
                    lax.dot_general(
                        scaled[j, sl, :], out[j, sl, :], (((0,), (0,)), ((), ())), preferred_element_type=F32
                    )
                )
            for b in range(2):
                h = 2 * j + b
                one = slice(b * HD, (b + 1) * HD)
                sums = [m[one, one] for m in both]
                s1_out[pl.ds(h * HD, HD), :] = sums[0]
                sv[h // group, pl.ds(h % group * HD, HD), :] = (
                    sums[0] * ends[1:2, h : h + 1] + sums[1]
                ).astype(BF16)
    for p in range(n_y):
        log = shard[...] if p == 0 else pltpu.roll(shard[...], HD - p * group, 1)
        sv[p, pl.ds(group * HD, LOG_ROWS), :] = log_rows(log)
    for d in range(n_y):
        messages[d][...] = sv[place_along_y(n_y, d)]


def key_value(n_y, far, w, total, ek, ends, shard, after):
    _, n_tiles, rows, _ = total.shape
    width = w.shape[2]
    depth = far[0].shape[1]
    size = (width // n_y + LOG_ROWS, HD)
    tiles = like(BF16, n_tiles, rows, TILE)
    return call(
        functools.partial(key_value_kernel, n_y),
        "key_value",
        (*far, w, total, ek, ends, shard, after),
        [tiles, tiles, like(F32, width, HD)] + [like(BF16, *size)] * n_y,
        16,
        4 * rows * 2 * depth * width,
        8 * rows * width + 8 * depth * width,
        scratch=[
            pltpu.VMEM((rows, 2 * depth), BF16),
            pltpu.VMEM((n_tiles, rows, TILE), BF16),
            pltpu.VMEM((n_y, *size), BF16),
        ],
    )


def query_kernel(f0, f1, w, total, q_out, x):
    depth = f0.shape[1]
    for i, f in enumerate((f0, f1)):
        x[:, i * depth : (i + 1) * depth] = f[...]
    for j in range(q_out.shape[0]):
        q_out[j] = silu(total[0, j] + dot(x[...], w[0, :, pl.ds(j * TILE, TILE)])).astype(BF16)


def query(far, w, total):
    _, n_tiles, rows, _ = total.shape
    depth = 2 * far[0].shape[1]
    return call(
        query_kernel,
        "query",
        (*far, w, total),
        [like(BF16, n_tiles, rows, TILE)],
        12,
        2 * rows * depth * n_tiles * TILE,
        6 * rows * n_tiles * TILE,
        scratch=[pltpu.VMEM((rows, depth), BF16)],
    )[0]


def inner_kernel(q, k, v, acol, arow, ea, qs_out, o_out, mark):
    mark[...] = jnp.zeros_like(mark)
    n_tiles, rows, _ = q.shape
    t = lax.broadcasted_iota(jnp.int32, (CHUNK, CHUNK), 0)
    s = lax.broadcasted_iota(jnp.int32, (CHUNK, CHUNK), 1)
    causal = s <= t
    for j in range(n_tiles):
        for b in range(2):
            h = 2 * j + b
            one = pl.ds(b * HD, HD)
            for c in range(rows // CHUNK):
                sl = pl.ds(c * CHUNK, CHUNK)
                scores = lax.dot_general(
                    q[j, sl, one], k[j, sl, one], (((1,), (1,)), ((), ())), preferred_element_type=F32
                )
                spread = acol[sl, h : h + 1] - arow[h : h + 1, sl]
                weighted = jnp.where(causal, scores * jnp.exp(jnp.minimum(spread, 0.0)), 0.0)
                o_out[j, sl, one] = dot(weighted.astype(BF16), v[j, sl, one])
                qs_out[j, sl, one] = (q[j, sl, one].astype(F32) * ea[sl, h : h + 1]).astype(BF16)


def inner(q, k, v, acol, arow, ea):
    n_tiles, rows, _ = k.shape
    tiles = (n_tiles, rows, TILE)
    return call(
        inner_kernel,
        "inner",
        (q, k, v, acol, arow, ea),
        [like(BF16, *tiles), like(F32, *tiles), MARK],
        16,
        4 * rows * CHUNK * n_tiles * TILE,
        14 * rows * n_tiles * TILE,
    )


def sum_logs(choose, logs):
    total = jnp.zeros_like(logs[0])
    for y, log in enumerate(logs):
        total = total + jnp.where(choose(y), log, 0.0)
    return total


def row_kernel(n_y, *refs):
    messages, (mark, out, done) = refs[:n_y], refs[n_y:]
    done[...] = mark[...]
    at = [place_along_y(n_y, -d) for d in (0, *send_order(n_y))]
    logs = [log_of(m) for m in messages]
    weights = [jnp.exp(sum_logs(lambda e: at[e] > at[d], logs)) for d in range(n_y)]
    for h in range(out.shape[0] // HD):
        one = pl.ds(h * HD, HD)
        total = None
        for weight, m in zip(weights, messages):
            term = m[one, :].astype(F32) * weight[:, h : h + 1]
            total = term if total is None else total + term
        out[one, :] = total.astype(BF16)
    out[pl.ds(out.shape[0] - LOG_ROWS, LOG_ROWS), :] = log_rows(sum(logs[1:], logs[0]))


def row_sum(messages, after):
    size = messages[0].shape
    n = len(messages)
    return call(
        functools.partial(row_kernel, n),
        "row_sum",
        (*messages, after),
        [like(BF16, *size), MARK],
        4,
        8 * size[0] * HD,
        16 * size[0] * HD,
    )


def state_kernel(n_y, n_z, *refs):
    messages, earlier, outs = refs[:n_y], refs[n_y : n_y + n_z - 1], refs[n_y + n_z :]
    my_z = lax.axis_index("seq") // n_y
    at = [place_along_y(n_y, -d) for d in (0, *send_order(n_y))]
    logs = [log_of(m) for m in messages]
    gap = jnp.zeros_like(logs[0])
    from_rows = []
    earlier = earlier[::-1]
    for e in range(1, n_z):
        from_rows.append(jnp.where(e <= my_z, jnp.exp(gap), 0.0))
        gap = gap + log_of(earlier[e - 1])
    for d in range(n_y):
        there = place_along_y(n_y, d)
        start = jnp.exp(sum_logs(lambda e: at[e] < there, logs))
        weights = [
            jnp.where(at[s] < there, jnp.exp(sum_logs(lambda e: (at[e] > at[s]) & (at[e] < there), logs)), 0.0)
            for s in range(n_y)
        ]
        for h in range(outs[d].shape[0] // HD):
            one = pl.ds(h * HD, HD)
            state = jnp.zeros((HD, HD), F32)
            for weight, m in zip(from_rows, earlier):
                state = state + m[one, :].astype(F32) * (weight[:, h : h + 1] * start[:, h : h + 1])
            for weight, m in zip(weights, messages):
                state = state + m[one, :].astype(F32) * weight[:, h : h + 1]
            outs[d][one, :] = state.astype(BF16)


def states(messages, earlier, after):
    n_y, n_z = len(messages), len(earlier) + 1
    rows = messages[0].shape[0] - LOG_ROWS
    return call(
        functools.partial(state_kernel, n_y, n_z),
        "states",
        (*messages, *earlier, after),
        [like(BF16, rows, HD)] * n_y,
        4,
        64 * rows * HD,
        24 * rows * HD,
    )


def fetch_kernel(shifts, w, after, out, done, sems):
    copies = Copies(sems)
    slice_width = out.shape[2]
    reads = []
    for i, shift in enumerate(shifts):
        start = pl.multiple_of(tensor_at(shift) * slice_width, HD)
        reads.append(copies.start(w.at[:, pl.ds(start, slice_width)], out.at[i]))
    done[...] = jnp.zeros_like(done)
    for r in reads:
        r.wait()


def fetch_out(shifts, w_out, slice_width, after):
    n = len(shifts)
    return call(
        functools.partial(fetch_kernel, shifts),
        "fetch_out",
        (w_out, after),
        [like(BF16, n, w_out.shape[0], slice_width), MARK],
        4,
        0,
        2 * w_out.size,
        scratch=[pltpu.SemaphoreType.DMA((n,))],
        big=(0,),
        loose=(1,),
    )


def attend_kernel(n_y, qs, o, w, s1, ends, *refs):
    received, (attn, top, bot, state) = refs[:n_y], refs[n_y:]
    half, slice_width = top.shape
    n_tiles = qs.shape[0]
    size = received[0].shape[0]
    for d, block in zip((0, *send_order(n_y)), received):
        row = pl.multiple_of(place_along_y(n_y, -d) * size, HD)
        state[pl.ds(row, size), :] = block[...]
    for j in range(n_tiles):
        for b in range(2):
            h = 2 * j + b
            cols = pl.ds(h * HD, HD)
            one = pl.ds(b * HD, HD)
            first = state[cols, :]
            second = (first.astype(F32) * ends[0:1, h : h + 1] + s1[cols, :]).astype(BF16)
            for c, held in ((0, first), (1, second)):
                sl = pl.ds(c * CHUNK, CHUNK)
                out = o[j, sl, one] + dot(qs[j, sl, one], held)
                mean = jnp.mean(out * out, axis=1, keepdims=True)
                attn[sl, cols] = (out * lax.rsqrt(mean + 1e-6)).astype(BF16)
    for j in range(slice_width // TILE):
        cols = pl.ds(j * TILE, TILE)
        out = dot(attn[...], w[0, :, cols]).astype(BF16)
        top[:, cols] = out[:half]
        bot[:, cols] = out[half:]


def attend(n_y, qs, o, w_out, s1, ends, received, slice_width):
    n_tiles, rows, _ = qs.shape
    width = n_tiles * TILE
    half = rows // 2
    return call(
        functools.partial(attend_kernel, n_y),
        "attend",
        (qs, o, w_out, s1, ends, *received),
        [like(BF16, rows, width), like(BF16, half, slice_width), like(BF16, half, slice_width)],
        16,
        2 * rows * width * (HD + slice_width),
        rows * width * 8 + width * slice_width * 2,
        scratch=[pltpu.VMEM((width, HD), BF16)],
    )


def output_kernel(attn, w, p_top, p_bot, m_top, m_bot, own):
    half, slice_width = p_top.shape
    for i, outs in enumerate(((p_top, p_bot), (m_top, m_bot), (own,))):
        for j in range(slice_width // TILE):
            cols = pl.ds(j * TILE, TILE)
            out = dot(attn[...], w[i + 1, :, cols]).astype(BF16)
            if len(outs) == 1:
                own[:, cols] = out
            else:
                outs[0][:, cols] = out[:half]
                outs[1][:, cols] = out[half:]


def output(attn, w_out, slice_width):
    rows, width = attn.shape
    half = rows // 2
    return call(
        output_kernel,
        "output",
        (attn, w_out),
        [like(BF16, half, slice_width)] * 4 + [like(BF16, rows, slice_width)],
        16,
        6 * rows * width * slice_width,
        6 * width * slice_width + 8 * rows * slice_width,
    )


def finish_kernel(own, lt, lb, rt, rb, out):
    half = lt.shape[0]
    for i, (a, b) in enumerate(((lt, rt), (lb, rb))):
        sl = pl.ds(i * half, half)
        out[sl, :] = (own[sl, :].astype(F32) + a[...].astype(F32) + b[...].astype(F32)).astype(BF16)


def finish(*parts):
    own = parts[0]
    return call(finish_kernel, "finish", parts, [like(BF16, *own.shape)], 8, own.size * 2, own.size * 8)[0]


def body(n_y, tokens, w_qkv, log_decay, w_out):
    slice_width = tokens.shape[1]
    n_t = lax.axis_size("tensor")
    n_z = lax.axis_size("seq") // n_y

    def along_x(x, shift):
        return lax.ppermute(x, "tensor", [(i, (i + shift) % n_t) for i in range(n_t)])

    def along_y(x, shift):
        return lax.ppermute(
            x, "seq", [(z * n_y + y, z * n_y + (y + shift) % n_y) for z in range(n_z) for y in range(n_y)]
        )

    def along_z(x, shift):
        return lax.ppermute(
            x, "seq", [(z * n_y + y, (z + shift) % n_z * n_y + y) for z in range(n_z) for y in range(n_y)]
        )

    w = w_qkv.transpose(1, 0, 2)
    t0, t1, early = split(tokens, w)

    l0 = along_x(t0, 1)
    r1 = along_x(t1, -1)
    l1 = along_x(t1, 1)
    r0 = along_x(t0, -1)
    f0 = along_x(l0, 1)
    f1 = along_x(r1, -1)

    arow, acol, ek, ea, ends, shard = decays(log_decay)
    far_places = ((2, 0), (2, 1))
    side_places = ((-1, 1), (1, 0))
    total = own_products(t0, t1, w, early)
    total, w_side = near(((-1, 0), (1, 1)), (l0, r1), w, total, ahead=side_places)
    total, w_far = near(side_places, (l1, r0), w, total, w_side, ahead=far_places)
    far = (f0, f1)
    w_slices, mark = fetch_out((2, 1, -1, 0), w_out, slice_width, total)
    k, v, s1, *kvs = key_value(n_y, far, w_far, total, ek, ends, shard, mark)

    sums = [kvs[0]] + [along_y(kvs[d], d) for d in send_order(n_y)]
    q = query(far, w_far, total)
    qs, o, mark = inner(q, k, v, acol, arow, ea)
    row, mark = row_sum(sums, mark)
    earlier = [along_z(row, e) for e in send_order(n_z)]
    starts = states(sums, earlier, mark)
    received = [starts[0]] + [along_y(starts[d], d) for d in send_order(n_y)]

    attn, far_top, far_bot = attend(n_y, qs, o, w_slices, s1, ends, received, slice_width)
    relay_top = along_x(far_top, 1)
    relay_bot = along_x(far_bot, -1)
    p_top, p_bot, m_top, m_bot, own = output(attn, w_slices, slice_width)
    left_bot = along_x(p_bot, 1)
    right_top = along_x(m_top, -1)
    left_top = along_x(p_top + relay_top, 1)
    right_bot = along_x(m_bot + relay_bot, -1)
    return finish(own, left_top, left_bot, right_top, right_bot)


def solution(mesh):
    in_specs = (
        P(("dp", "seq"), "tensor"),
        P(None, None, "tensor"),
        P("tensor", ("dp", "seq")),
        P("tensor", None),
    )
    out_specs = P(("dp", "seq"), "tensor")
    n_seq = mesh.shape["seq"]
    n_y = 4 if n_seq % 4 == 0 else 1
    return jax.shard_map(
        functools.partial(body, n_y), mesh=mesh, in_specs=in_specs, out_specs=out_specs, check_vma=False
    )
```

```python
import functools

import jax
import jax.numpy as jnp
from jax import lax
from jax.experimental import pallas as pl
from jax.experimental.pallas import tpu as pltpu
from jax.sharding import PartitionSpec as P

BF16 = jnp.bfloat16
F32 = jnp.float32
HD = 128
TILE = 2 * HD
CHUNK = 256
LOG_ROWS = 16
MIB = 1024 * 1024

ANY = pl.BlockSpec(memory_space=pl.ANY)
HBM = pl.BlockSpec(memory_space=pltpu.HBM)


def dot(a, b):
    return jnp.dot(a, b, preferred_element_type=F32)


def exact_dot(a, b):
    return jnp.dot(a, b, preferred_element_type=F32, precision=lax.Precision.HIGHEST)


def silu(x):
    half = 0.5 * x
    return half + half * jnp.tanh(half)


def whole(x):
    return pl.BlockSpec(x.shape, lambda i: (0,) * len(x.shape))


def like(dtype, *shape):
    return jax.ShapeDtypeStruct(shape, dtype)


def call(kernel, name, args, outs, mib, flops, nbytes, scratch=(), big=(), big_outs=(), aliases=None, loose=()):
    args = [pltpu.with_memory_space_constraint(a, pltpu.HBM) if i in big else a for i, a in enumerate(args)]
    return pl.pallas_call(
        kernel,
        grid=(1,),
        in_specs=[HBM if i in big else ANY if i in loose else whole(a) for i, a in enumerate(args)],
        out_specs=[HBM if i in big_outs else whole(a) for i, a in enumerate(outs)],
        out_shape=[pltpu.HBM(a.shape, a.dtype) if i in big_outs else a for i, a in enumerate(outs)],
        scratch_shapes=list(scratch),
        input_output_aliases=aliases or {},
        compiler_params=pltpu.CompilerParams(vmem_limit_bytes=mib * MIB),
        cost_estimate=pl.CostEstimate(flops=int(flops), bytes_accessed=int(nbytes), transcendentals=0),
        name=name,
    )(*args)


MARK = like(F32, 8, HD)


class Copies:
    def __init__(self, sems):
        self.sems, self.used = sems, 0

    def start(self, src, dst):
        copy = pltpu.make_async_copy(src, dst, self.sems.at[self.used])
        self.used += 1
        copy.start()
        return copy


class Stages:
    def __init__(self, copies, groups, ahead=2):
        self.copies, self.groups, self.ahead = copies, groups, ahead
        self.running = []
        for _ in range(min(ahead, len(groups))):
            self.begin()

    def begin(self):
        if len(self.running) < len(self.groups):
            self.running.append([self.copies.start(*pair) for pair in self.groups[len(self.running)]])

    def take(self, i):
        for r in self.running[i]:
            r.wait()
        self.begin()


def tensor_at(shift):
    n = lax.axis_size("tensor")
    return lax.rem(lax.axis_index("tensor") + (shift + n), n)


def decay_kernel(ld, ldt, after, arow, acol, ek, ea, ends, shard):
    heads, rows = ld.shape
    r = lax.broadcasted_iota(jnp.int32, (CHUNK, CHUNK), 0)
    c = lax.broadcasted_iota(jnp.int32, (CHUNK, CHUNK), 1)
    lower = (c <= r).astype(F32)
    upper = (r <= c).astype(F32)
    total = jnp.zeros((1, heads), F32)
    for i in range(rows // CHUNK):
        sl = pl.ds(i * CHUNK, CHUNK)
        down = exact_dot(lower, ldt[sl, :])
        end = down[CHUNK - 1 : CHUNK, :]
        arow[:, sl] = exact_dot(ld[:, sl], upper)
        acol[sl, :] = down
        ek[sl, :] = jnp.exp(jnp.minimum(end - down, 0.0))
        ea[sl, :] = jnp.exp(jnp.minimum(down, 0.0))
        ends[i : i + 1, :] = jnp.exp(jnp.minimum(end, 0.0))
        total = total + end
    shard[...] = jnp.zeros_like(shard)
    shard[0:1, 0:heads] = jnp.minimum(total, 0.0)


def decays(log_decay, after):
    heads, rows = log_decay.shape
    outs = [like(F32, heads, rows)] + [like(F32, rows, heads)] * 3
    outs += [like(F32, rows // CHUNK, heads), like(F32, 1, HD)]
    return call(decay_kernel, "decays", (log_decay, log_decay.T, after), outs, 4, 0, 1e5, loose=(2,))


def piece_rows(w, part, place, depth):
    shift, half = place
    row = pl.multiple_of((tensor_at(shift) * 2 + half) * depth, HD)
    return w.at[part, pl.ds(row, depth), :]


def near_kernel(places, ahead, has_before, has_weights, a, b, w, *refs):
    refs = list(refs)
    before = refs.pop(0) if has_before else None
    held = refs.pop(0) if has_weights else None
    total = refs.pop(0)
    fetched = refs.pop(0) if ahead else None
    x, *wv, sems = refs
    depth = a.shape[1]
    parts = w.shape[0]
    copies = Copies(sems)

    def rows_of(part, two, to):
        return [(piece_rows(w, part, place, depth), to.at[part, pl.ds(m * depth, depth), :]) for m, place in enumerate(two)]

    groups = [] if has_weights else [rows_of(p, places, wv[0]) for p in range(parts)]
    if ahead:
        groups += [rows_of(p, ahead, fetched) for p in range(parts)]
    stages = Stages(copies, groups, 3)
    x[:, :depth] = a[...]
    x[:, depth:] = b[...]
    for p in range(parts):
        if not has_weights:
            stages.take(p)
        source = held if has_weights else wv[0]
        for j in range(total.shape[1]):
            term = dot(x[...], source[p, :, pl.ds(j * TILE, TILE)])
            total[p, j] = before[p, j] + term if has_before else term
    if ahead:
        for p in range(parts):
            stages.take(p if has_weights else parts + p)


def near(places, two, w, before=None, held=None, ahead=None):
    rows, depth = two[0].shape
    parts, _, width = w.shape
    outs = [like(F32, parts, width // TILE, rows, TILE)]
    block = (parts, 2 * depth, width)
    if ahead:
        outs.append(like(BF16, *block))
    return call(
        functools.partial(near_kernel, places, ahead, before is not None, held is not None),
        "near",
        [*two, w] + [m for m in (before, held) if m is not None],
        outs,
        12 if held is None else 4,
        4 * rows * depth * parts * width,
        4 * depth * parts * width + rows * parts * width * 4,
        scratch=[pltpu.VMEM((rows, 2 * depth), BF16)]
        + ([] if held is not None else [pltpu.VMEM(block, BF16)])
        + [pltpu.SemaphoreType.DMA((4 * parts,))],
        big=(2,),
    )


def split_kernel(tokens, w, t0, t1, early, x, wv, tv, sems):
    depth = t0.shape[1]
    parts = w.shape[0]
    copies = Copies(sems)
    reads = [copies.start(tokens.at[:, pl.ds(m * depth, depth)], t) for m, t in enumerate((t0, t1))]
    first = lax.axis_index("dp") == 0
    later = Copies(sems.at[pl.ds(2, parts + parts * tv.shape[1])])

    @pl.when(first)
    def _():
        row = pl.multiple_of(tensor_at(0) * 2 * depth, HD)
        fetches = [later.start(w.at[p, pl.ds(row, 2 * depth), :], wv.at[p]) for p in range(parts)]
        for r in reads:
            r.wait()
        x[:, :depth] = t0[...]
        x[:, depth:] = t1[...]
        writes = []
        for p in range(parts):
            fetches[p].wait()
            for j in range(tv.shape[1]):
                tv[p, j] = dot(x[...], wv[p, :, pl.ds(j * TILE, TILE)])
                writes.append(later.start(tv.at[p, j], early.at[p, j]))
        for r in writes:
            r.wait()

    @pl.when(jnp.logical_not(first))
    def _():
        for r in reads:
            r.wait()


def split(tokens, w):
    rows, width = tokens.shape
    parts, _, columns = w.shape
    block = (parts, columns // TILE, rows, TILE)
    return call(
        split_kernel,
        "split",
        (tokens, w),
        [like(BF16, rows, width // 2)] * 2 + [like(F32, *block)],
        16,
        2 * rows * width * parts * columns,
        2 * width * parts * columns,
        scratch=[
            pltpu.VMEM((rows, width), BF16),
            pltpu.VMEM((parts, width, columns), BF16),
            pltpu.VMEM(block, F32),
            pltpu.SemaphoreType.DMA((2 + parts + parts * block[1],)),
        ],
        big=range(2),
        big_outs=(2,),
    )


def own_kernel(shifts, t0, t1, w, early, w_out, total, slices, x, wv, sems):
    depth = t0.shape[1]
    parts = w.shape[0]
    columns = slices.shape[2]
    copies = Copies(sems)
    first = lax.axis_index("dp") == 0

    def fetch_slices():
        reads = []
        for i, shift in enumerate(shifts):
            start = pl.multiple_of(tensor_at(shift) * columns, HD)
            reads.append(copies.start(w_out.at[:, pl.ds(start, columns)], slices.at[i]))
        return reads

    @pl.when(first)
    def _():
        copy = copies.start(early, total)
        reads = fetch_slices()
        copy.wait()
        for r in reads:
            r.wait()

    @pl.when(jnp.logical_not(first))
    def _():
        copies.used = 0
        row = pl.multiple_of(tensor_at(0) * 2 * depth, HD)
        fetches = [copies.start(w.at[p, pl.ds(row, 2 * depth), :], wv.at[p]) for p in range(parts)]
        x[:, :depth] = t0[...]
        x[:, depth:] = t1[...]
        for p in range(parts):
            fetches[p].wait()
            if p == 0:
                reads = fetch_slices()
            for j in range(total.shape[1]):
                total[p, j] = dot(x[...], wv[p, :, pl.ds(j * TILE, TILE)])
        for r in reads:
            r.wait()


def own_products(t0, t1, w, early, w_out):
    rows, depth = t0.shape
    parts, _, columns = w.shape
    shifts = (2, 1, -1, 0)
    return call(
        functools.partial(own_kernel, shifts),
        "own",
        (t0, t1, w, early, w_out),
        [like(F32, *early.shape), like(BF16, len(shifts), w_out.shape[0], 2 * depth)],
        12,
        4 * rows * depth * parts * columns,
        4 * depth * parts * columns + 2 * w_out.size,
        scratch=[
            pltpu.VMEM((rows, 2 * depth), BF16),
            pltpu.VMEM((parts, 2 * depth, columns), BF16),
            pltpu.SemaphoreType.DMA((parts + 1 + len(shifts),)),
        ],
        big=(2, 3, 4),
    )


def log_rows(log):
    high = log.astype(BF16).astype(F32)
    middle = (log - high).astype(BF16).astype(F32)
    low = log - high - middle
    row = lax.broadcasted_iota(jnp.int32, (LOG_ROWS, HD), 0)
    rows = jnp.where(row == 0, high, jnp.where(row == 1, middle, low))
    return jnp.where(row < 3, rows, 0.0).astype(BF16)


def log_of(message):
    tail = message[pl.ds(message.shape[0] - LOG_ROWS, LOG_ROWS), :].astype(F32)
    return jnp.minimum(tail[0:1] + tail[1:2] + tail[2:3], 0.0)


def send_order(n):
    return range(n - 1, 0, -1)


def place_along_y(n_y, shift=0):
    return lax.rem(lax.axis_index("seq") + (shift + n_y), n_y)


def key_value_kernel(n_y, f0, f1, w, total, ek, ends, shard, k_out, v_out, s1_out, *refs):
    messages, (x, scaled, sv) = refs[:n_y], refs[n_y:]
    n_tiles, rows, _ = k_out.shape
    depth = f0.shape[1]
    for i, f in enumerate((f0, f1)):
        x[:, i * depth : (i + 1) * depth] = f[...]
    group = n_tiles * 2 // n_y
    for i, out in enumerate((k_out, v_out)):
        for j in range(n_tiles):
            made = silu(total[i + 1, j] + dot(x[...], w[i + 1, :, pl.ds(j * TILE, TILE)])).astype(BF16)
            out[j] = made
            if i == 0:
                for b in range(2):
                    key = made[:, b * HD : (b + 1) * HD].astype(F32)
                    scaled[j, :, pl.ds(b * HD, HD)] = (key * ek[:, 2 * j + b : 2 * j + b + 1]).astype(BF16)
                continue
            both = []
            for c in range(rows // CHUNK):
                sl = pl.ds(c * CHUNK, CHUNK)
                both.append(
                    lax.dot_general(
                        scaled[j, sl, :], out[j, sl, :], (((0,), (0,)), ((), ())), preferred_element_type=F32
                    )
                )
            for b in range(2):
                h = 2 * j + b
                one = slice(b * HD, (b + 1) * HD)
                sums = [m[one, one] for m in both]
                s1_out[pl.ds(h * HD, HD), :] = sums[0]
                sv[h // group, pl.ds(h % group * HD, HD), :] = (
                    sums[0] * ends[1:2, h : h + 1] + sums[1]
                ).astype(BF16)
    for p in range(n_y):
        log = shard[...] if p == 0 else pltpu.roll(shard[...], HD - p * group, 1)
        sv[p, pl.ds(group * HD, LOG_ROWS), :] = log_rows(log)
    for d in range(n_y):
        messages[d][...] = sv[place_along_y(n_y, d)]


def key_value(n_y, far, w, total, ek, ends, shard):
    _, n_tiles, rows, _ = total.shape
    width = w.shape[2]
    depth = far[0].shape[1]
    size = (width // n_y + LOG_ROWS, HD)
    tiles = like(BF16, n_tiles, rows, TILE)
    return call(
        functools.partial(key_value_kernel, n_y),
        "key_value",
        (*far, w, total, ek, ends, shard),
        [tiles, tiles, like(F32, width, HD)] + [like(BF16, *size)] * n_y,
        16,
        4 * rows * 2 * depth * width,
        8 * rows * width + 8 * depth * width,
        scratch=[
            pltpu.VMEM((rows, 2 * depth), BF16),
            pltpu.VMEM((n_tiles, rows, TILE), BF16),
            pltpu.VMEM((n_y, *size), BF16),
        ],
    )


def query_kernel(f0, f1, w, total, q_out, x):
    depth = f0.shape[1]
    for i, f in enumerate((f0, f1)):
        x[:, i * depth : (i + 1) * depth] = f[...]
    for j in range(q_out.shape[0]):
        q_out[j] = silu(total[0, j] + dot(x[...], w[0, :, pl.ds(j * TILE, TILE)])).astype(BF16)


def query(far, w, total):
    _, n_tiles, rows, _ = total.shape
    depth = 2 * far[0].shape[1]
    return call(
        query_kernel,
        "query",
        (*far, w, total),
        [like(BF16, n_tiles, rows, TILE)],
        12,
        2 * rows * depth * n_tiles * TILE,
        6 * rows * n_tiles * TILE,
        scratch=[pltpu.VMEM((rows, depth), BF16)],
    )[0]


def inner_kernel(q, k, v, acol, arow, ea, qs_out, o_out, mark):
    mark[...] = jnp.zeros_like(mark)
    n_tiles, rows, _ = q.shape
    t = lax.broadcasted_iota(jnp.int32, (CHUNK, CHUNK), 0)
    s = lax.broadcasted_iota(jnp.int32, (CHUNK, CHUNK), 1)
    causal = s <= t
    for j in range(n_tiles):
        for b in range(2):
            h = 2 * j + b
            one = pl.ds(b * HD, HD)
            for c in range(rows // CHUNK):
                sl = pl.ds(c * CHUNK, CHUNK)
                scores = lax.dot_general(
                    q[j, sl, one], k[j, sl, one], (((1,), (1,)), ((), ())), preferred_element_type=F32
                )
                spread = acol[sl, h : h + 1] - arow[h : h + 1, sl]
                weighted = jnp.where(causal, scores * jnp.exp(jnp.minimum(spread, 0.0)), 0.0)
                o_out[j, sl, one] = dot(weighted.astype(BF16), v[j, sl, one])
                qs_out[j, sl, one] = (q[j, sl, one].astype(F32) * ea[sl, h : h + 1]).astype(BF16)


def inner(q, k, v, acol, arow, ea):
    n_tiles, rows, _ = k.shape
    tiles = (n_tiles, rows, TILE)
    return call(
        inner_kernel,
        "inner",
        (q, k, v, acol, arow, ea),
        [like(BF16, *tiles), like(F32, *tiles), MARK],
        16,
        4 * rows * CHUNK * n_tiles * TILE,
        14 * rows * n_tiles * TILE,
    )


def sum_logs(choose, logs):
    total = jnp.zeros_like(logs[0])
    for y, log in enumerate(logs):
        total = total + jnp.where(choose(y), log, 0.0)
    return total


def row_kernel(n_y, *refs):
    messages, (mark, out, done) = refs[:n_y], refs[n_y:]
    done[...] = mark[...]
    at = [place_along_y(n_y, -d) for d in (0, *send_order(n_y))]
    logs = [log_of(m) for m in messages]
    weights = [jnp.exp(sum_logs(lambda e: at[e] > at[d], logs)) for d in range(n_y)]
    for h in range(out.shape[0] // HD):
        one = pl.ds(h * HD, HD)
        total = None
        for weight, m in zip(weights, messages):
            term = m[one, :].astype(F32) * weight[:, h : h + 1]
            total = term if total is None else total + term
        out[one, :] = total.astype(BF16)
    out[pl.ds(out.shape[0] - LOG_ROWS, LOG_ROWS), :] = log_rows(sum(logs[1:], logs[0]))


def row_sum(messages, after):
    size = messages[0].shape
    n = len(messages)
    return call(
        functools.partial(row_kernel, n),
        "row_sum",
        (*messages, after),
        [like(BF16, *size), MARK],
        4,
        8 * size[0] * HD,
        16 * size[0] * HD,
    )


def state_kernel(n_y, n_z, *refs):
    messages, earlier, outs = refs[:n_y], refs[n_y : n_y + n_z - 1], refs[n_y + n_z :]
    my_z = lax.axis_index("seq") // n_y
    at = [place_along_y(n_y, -d) for d in (0, *send_order(n_y))]
    logs = [log_of(m) for m in messages]
    gap = jnp.zeros_like(logs[0])
    from_rows = []
    earlier = earlier[::-1]
    for e in range(1, n_z):
        from_rows.append(jnp.where(e <= my_z, jnp.exp(gap), 0.0))
        gap = gap + log_of(earlier[e - 1])
    for d in range(n_y):
        there = place_along_y(n_y, d)
        start = jnp.exp(sum_logs(lambda e: at[e] < there, logs))
        weights = [
            jnp.where(at[s] < there, jnp.exp(sum_logs(lambda e: (at[e] > at[s]) & (at[e] < there), logs)), 0.0)
            for s in range(n_y)
        ]
        for h in range(outs[d].shape[0] // HD):
            one = pl.ds(h * HD, HD)
            state = jnp.zeros((HD, HD), F32)
            for weight, m in zip(from_rows, earlier):
                state = state + m[one, :].astype(F32) * (weight[:, h : h + 1] * start[:, h : h + 1])
            for weight, m in zip(weights, messages):
                state = state + m[one, :].astype(F32) * weight[:, h : h + 1]
            outs[d][one, :] = state.astype(BF16)


def states(messages, earlier, after):
    n_y, n_z = len(messages), len(earlier) + 1
    rows = messages[0].shape[0] - LOG_ROWS
    return call(
        functools.partial(state_kernel, n_y, n_z),
        "states",
        (*messages, *earlier, after),
        [like(BF16, rows, HD)] * n_y,
        4,
        64 * rows * HD,
        24 * rows * HD,
    )


def attend_kernel(n_y, qs, o, w, s1, ends, *refs):
    received, (attn, top, bot, state) = refs[:n_y], refs[n_y:]
    half, slice_width = top.shape
    n_tiles = qs.shape[0]
    size = received[0].shape[0]
    for d, block in zip((0, *send_order(n_y)), received):
        row = pl.multiple_of(place_along_y(n_y, -d) * size, HD)
        state[pl.ds(row, size), :] = block[...]
    for j in range(n_tiles):
        for b in range(2):
            h = 2 * j + b
            cols = pl.ds(h * HD, HD)
            one = pl.ds(b * HD, HD)
            first = state[cols, :]
            second = (first.astype(F32) * ends[0:1, h : h + 1] + s1[cols, :]).astype(BF16)
            for c, held in ((0, first), (1, second)):
                sl = pl.ds(c * CHUNK, CHUNK)
                out = o[j, sl, one] + dot(qs[j, sl, one], held)
                mean = jnp.mean(out * out, axis=1, keepdims=True)
                attn[sl, cols] = (out * lax.rsqrt(mean + 1e-6)).astype(BF16)
    for j in range(slice_width // TILE):
        cols = pl.ds(j * TILE, TILE)
        out = dot(attn[...], w[0, :, cols]).astype(BF16)
        top[:, cols] = out[:half]
        bot[:, cols] = out[half:]


def attend(n_y, qs, o, w_out, s1, ends, received, slice_width):
    n_tiles, rows, _ = qs.shape
    width = n_tiles * TILE
    half = rows // 2
    return call(
        functools.partial(attend_kernel, n_y),
        "attend",
        (qs, o, w_out, s1, ends, *received),
        [like(BF16, rows, width), like(BF16, half, slice_width), like(BF16, half, slice_width)],
        16,
        2 * rows * width * (HD + slice_width),
        rows * width * 8 + width * slice_width * 2,
        scratch=[pltpu.VMEM((width, HD), BF16)],
    )


def output_kernel(attn, w, p_top, p_bot, m_top, m_bot, own):
    half, slice_width = p_top.shape
    for i, outs in enumerate(((p_top, p_bot), (m_top, m_bot), (own,))):
        for j in range(slice_width // TILE):
            cols = pl.ds(j * TILE, TILE)
            out = dot(attn[...], w[i + 1, :, cols]).astype(BF16)
            if len(outs) == 1:
                own[:, cols] = out
            else:
                outs[0][:, cols] = out[:half]
                outs[1][:, cols] = out[half:]


def output(attn, w_out, slice_width):
    rows, width = attn.shape
    half = rows // 2
    return call(
        output_kernel,
        "output",
        (attn, w_out),
        [like(BF16, half, slice_width)] * 4 + [like(BF16, rows, slice_width)],
        16,
        6 * rows * width * slice_width,
        6 * width * slice_width + 8 * rows * slice_width,
    )


def finish_kernel(half, *refs):
    own, a, b, out, held, sem = (*refs[:3], *refs[-3:])
    rows = a.shape[0]
    sl = pl.ds(half * rows, rows)
    held[...] = (own[sl, :].astype(F32) + a[...].astype(F32) + b[...].astype(F32)).astype(BF16)
    copy = pltpu.make_async_copy(held, out.at[sl, :], sem)
    copy.start()
    copy.wait()


def finish(half, own, a, b, out=None):
    return call(
        functools.partial(finish_kernel, half),
        "finish",
        (own, a, b) if out is None else (own, a, b, out),
        [like(BF16, *own.shape)],
        8,
        own.size,
        own.size * 4,
        scratch=[pltpu.VMEM(a.shape, BF16), pltpu.SemaphoreType.DMA],
        big=(3,),
        big_outs=(0,),
        aliases=None if out is None else {3: 0},
    )[0]


def body(n_y, tokens, w_qkv, log_decay, w_out):
    slice_width = tokens.shape[1]
    n_t = lax.axis_size("tensor")
    n_z = lax.axis_size("seq") // n_y

    def along_x(x, shift):
        return lax.ppermute(x, "tensor", [(i, (i + shift) % n_t) for i in range(n_t)])

    def along_y(x, shift):
        return lax.ppermute(
            x, "seq", [(z * n_y + y, z * n_y + (y + shift) % n_y) for z in range(n_z) for y in range(n_y)]
        )

    def along_z(x, shift):
        return lax.ppermute(
            x, "seq", [(z * n_y + y, (z + shift) % n_z * n_y + y) for z in range(n_z) for y in range(n_y)]
        )

    w = w_qkv.transpose(1, 0, 2)
    t0, t1, early = split(tokens, w)

    l0 = along_x(t0, 1)
    r1 = along_x(t1, -1)
    l1 = along_x(t1, 1)
    r0 = along_x(t0, -1)
    f0 = along_x(l0, 1)
    f1 = along_x(r1, -1)

    far_places = ((2, 0), (2, 1))
    side_places = ((-1, 1), (1, 0))
    total, w_slices = own_products(t0, t1, w, early, w_out)
    total, w_side = near(((-1, 0), (1, 1)), (l0, r1), w, total, ahead=side_places)
    total, w_far = near(side_places, (l1, r0), w, total, w_side, ahead=far_places)
    arow, acol, ek, ea, ends, shard = decays(log_decay, total)
    far = (f0, f1)
    k, v, s1, *kvs = key_value(n_y, far, w_far, total, ek, ends, shard)

    sums = [kvs[0]] + [along_y(kvs[d], d) for d in send_order(n_y)]
    q = query(far, w_far, total)
    qs, o, mark = inner(q, k, v, acol, arow, ea)
    row, mark = row_sum(sums, mark)
    earlier = [along_z(row, e) for e in send_order(n_z)]
    starts = states(sums, earlier, mark)
    received = [starts[0]] + [along_y(starts[d], d) for d in send_order(n_y)]

    attn, far_top, far_bot = attend(n_y, qs, o, w_slices, s1, ends, received, slice_width)
    relay_top = along_x(far_top, 1)
    relay_bot = along_x(far_bot, -1)
    p_top, p_bot, m_top, m_bot, own = output(attn, w_slices, slice_width)
    left_bot = along_x(p_bot, 1)
    right_top = along_x(m_top, -1)
    left_top = along_x(p_top + relay_top, 1)
    right_bot = along_x(m_bot + relay_bot, -1)
    out = finish(1, own, left_bot, right_bot)
    return finish(0, own, left_top, right_top, out)


def solution(mesh):
    in_specs = (
        P(("dp", "seq"), "tensor"),
        P(None, None, "tensor"),
        P("tensor", ("dp", "seq")),
        P("tensor", None),
    )
    out_specs = P(("dp", "seq"), "tensor")
    n_seq = mesh.shape["seq"]
    n_y = 4 if n_seq % 4 == 0 else 1
    return jax.shard_map(
        functools.partial(body, n_y), mesh=mesh, in_specs=in_specs, out_specs=out_specs, check_vma=False
    )
```

```python
import functools

import jax
import jax.numpy as jnp
from jax import lax
from jax.experimental import pallas as pl
from jax.experimental.pallas import tpu as pltpu
from jax.sharding import PartitionSpec as P

BF16 = jnp.bfloat16
F32 = jnp.float32
HD = 128
TILE = 2 * HD
CHUNK = 256
LOG_ROWS = 16
MIB = 1024 * 1024

ANY = pl.BlockSpec(memory_space=pl.ANY)
HBM = pl.BlockSpec(memory_space=pltpu.HBM)


def dot(a, b):
    return jnp.dot(a, b, preferred_element_type=F32)


def exact_dot(a, b):
    return jnp.dot(a, b, preferred_element_type=F32, precision=lax.Precision.HIGHEST)


def silu(x):
    half = 0.5 * x
    return half + half * jnp.tanh(half)


def whole(x):
    return pl.BlockSpec(x.shape, lambda i: (0,) * len(x.shape))


def like(dtype, *shape):
    return jax.ShapeDtypeStruct(shape, dtype)


def call(kernel, name, args, outs, mib, flops, nbytes, scratch=(), big=(), big_outs=(), aliases=None, loose=()):
    args = [pltpu.with_memory_space_constraint(a, pltpu.HBM) if i in big else a for i, a in enumerate(args)]
    return pl.pallas_call(
        kernel,
        grid=(1,),
        in_specs=[HBM if i in big else ANY if i in loose else whole(a) for i, a in enumerate(args)],
        out_specs=[HBM if i in big_outs else whole(a) for i, a in enumerate(outs)],
        out_shape=[pltpu.HBM(a.shape, a.dtype) if i in big_outs else a for i, a in enumerate(outs)],
        scratch_shapes=list(scratch),
        input_output_aliases=aliases or {},
        compiler_params=pltpu.CompilerParams(vmem_limit_bytes=mib * MIB),
        cost_estimate=pl.CostEstimate(flops=int(flops), bytes_accessed=int(nbytes), transcendentals=0),
        name=name,
    )(*args)


MARK = like(F32, 8, HD)


class Copies:
    def __init__(self, sems):
        self.sems, self.used = sems, 0

    def start(self, src, dst):
        copy = pltpu.make_async_copy(src, dst, self.sems.at[self.used])
        self.used += 1
        copy.start()
        return copy


class Stages:
    def __init__(self, copies, groups, ahead=2):
        self.copies, self.groups, self.ahead = copies, groups, ahead
        self.running = []
        for _ in range(min(ahead, len(groups))):
            self.begin()

    def begin(self):
        if len(self.running) < len(self.groups):
            self.running.append([self.copies.start(*pair) for pair in self.groups[len(self.running)]])

    def take(self, i):
        for r in self.running[i]:
            r.wait()
        self.begin()


def tensor_at(shift):
    n = lax.axis_size("tensor")
    return lax.rem(lax.axis_index("tensor") + (shift + n), n)


def decay_kernel(ld, ldt, after, arow, acol, ek, ea, ends, shard):
    heads, rows = ld.shape
    r = lax.broadcasted_iota(jnp.int32, (CHUNK, CHUNK), 0)
    c = lax.broadcasted_iota(jnp.int32, (CHUNK, CHUNK), 1)
    lower = (c <= r).astype(F32)
    upper = (r <= c).astype(F32)
    total = jnp.zeros((1, heads), F32)
    for i in range(rows // CHUNK):
        sl = pl.ds(i * CHUNK, CHUNK)
        down = exact_dot(lower, ldt[sl, :])
        end = down[CHUNK - 1 : CHUNK, :]
        arow[:, sl] = exact_dot(ld[:, sl], upper)
        acol[sl, :] = down
        ek[sl, :] = jnp.exp(jnp.minimum(end - down, 0.0))
        ea[sl, :] = jnp.exp(jnp.minimum(down, 0.0))
        ends[i : i + 1, :] = jnp.exp(jnp.minimum(end, 0.0))
        total = total + end
    shard[...] = jnp.zeros_like(shard)
    shard[0:1, 0:heads] = jnp.minimum(total, 0.0)


def decays(log_decay, after):
    heads, rows = log_decay.shape
    outs = [like(F32, heads, rows)] + [like(F32, rows, heads)] * 3
    outs += [like(F32, rows // CHUNK, heads), like(F32, 1, HD)]
    return call(decay_kernel, "decays", (log_decay, log_decay.T, after), outs, 4, 0, 1e5, loose=(2,))


def piece_rows(w, part, place, depth):
    shift, half = place
    row = pl.multiple_of((tensor_at(shift) * 2 + half) * depth, HD)
    return w.at[part, pl.ds(row, depth), :]


def near_kernel(places, ahead, has_before, has_weights, a, b, w, *refs):
    refs = list(refs)
    before = refs.pop(0) if has_before else None
    held = refs.pop(0) if has_weights else None
    total = refs.pop(0)
    fetched = refs.pop(0) if ahead else None
    x, *wv, sems = refs
    depth = a.shape[1]
    parts = w.shape[0]
    copies = Copies(sems)

    def rows_of(part, two, to):
        return [(piece_rows(w, part, place, depth), to.at[part, pl.ds(m * depth, depth), :]) for m, place in enumerate(two)]

    groups = [] if has_weights else [rows_of(p, places, wv[0]) for p in range(parts)]
    if ahead:
        groups += [rows_of(p, ahead, fetched) for p in range(parts)]
    stages = Stages(copies, groups, 3)
    x[:, :depth] = a[...]
    x[:, depth:] = b[...]
    for p in range(parts):
        if not has_weights:
            stages.take(p)
        source = held if has_weights else wv[0]
        for j in range(total.shape[1]):
            term = dot(x[...], source[p, :, pl.ds(j * TILE, TILE)])
            total[p, j] = before[p, j] + term if has_before else term
    if ahead:
        for p in range(parts):
            stages.take(p if has_weights else parts + p)


def near(places, two, w, before=None, held=None, ahead=None):
    rows, depth = two[0].shape
    parts, _, width = w.shape
    outs = [like(F32, parts, width // TILE, rows, TILE)]
    block = (parts, 2 * depth, width)
    if ahead:
        outs.append(like(BF16, *block))
    return call(
        functools.partial(near_kernel, places, ahead, before is not None, held is not None),
        "near",
        [*two, w] + [m for m in (before, held) if m is not None],
        outs,
        12 if held is None else 4,
        4 * rows * depth * parts * width,
        4 * depth * parts * width + rows * parts * width * 4,
        scratch=[pltpu.VMEM((rows, 2 * depth), BF16)]
        + ([] if held is not None else [pltpu.VMEM(block, BF16)])
        + [pltpu.SemaphoreType.DMA((4 * parts,))],
        big=(2,),
    )


def split_kernel(tokens, w, t0, t1, early, x, wv, tv, sems):
    depth = t0.shape[1]
    parts = w.shape[0]
    copies = Copies(sems)
    reads = [copies.start(tokens.at[:, pl.ds(m * depth, depth)], t) for m, t in enumerate((t0, t1))]
    first = lax.axis_index("dp") == 0
    later = Copies(sems.at[pl.ds(2, parts + parts * tv.shape[1])])

    @pl.when(first)
    def _():
        row = pl.multiple_of(tensor_at(0) * 2 * depth, HD)
        fetches = [later.start(w.at[p, pl.ds(row, 2 * depth), :], wv.at[p]) for p in range(parts)]
        for r in reads:
            r.wait()
        x[:, :depth] = t0[...]
        x[:, depth:] = t1[...]
        writes = []
        for p in range(parts):
            fetches[p].wait()
            for j in range(tv.shape[1]):
                tv[p, j] = dot(x[...], wv[p, :, pl.ds(j * TILE, TILE)])
                writes.append(later.start(tv.at[p, j], early.at[p, j]))
        for r in writes:
            r.wait()

    @pl.when(jnp.logical_not(first))
    def _():
        for r in reads:
            r.wait()


def split(tokens, w):
    rows, width = tokens.shape
    parts, _, columns = w.shape
    block = (parts, columns // TILE, rows, TILE)
    return call(
        split_kernel,
        "split",
        (tokens, w),
        [like(BF16, rows, width // 2)] * 2 + [like(F32, *block)],
        16,
        2 * rows * width * parts * columns,
        2 * width * parts * columns,
        scratch=[
            pltpu.VMEM((rows, width), BF16),
            pltpu.VMEM((parts, width, columns), BF16),
            pltpu.VMEM(block, F32),
            pltpu.SemaphoreType.DMA((2 + parts + parts * block[1],)),
        ],
        big=range(2),
        big_outs=(2,),
    )


def own_kernel(shifts, t0, t1, w, early, w_out, total, slices, x, wv, sems):
    depth = t0.shape[1]
    parts = w.shape[0]
    columns = slices.shape[2]
    copies = Copies(sems)
    first = lax.axis_index("dp") == 0

    def fetch_slices():
        reads = []
        for i, shift in enumerate(shifts):
            start = pl.multiple_of(tensor_at(shift) * columns, HD)
            reads.append(copies.start(w_out.at[:, pl.ds(start, columns)], slices.at[i]))
        return reads

    @pl.when(first)
    def _():
        copy = copies.start(early, total)
        reads = fetch_slices()
        copy.wait()
        for r in reads:
            r.wait()

    @pl.when(jnp.logical_not(first))
    def _():
        copies.used = 0
        row = pl.multiple_of(tensor_at(0) * 2 * depth, HD)
        fetches = [copies.start(w.at[p, pl.ds(row, 2 * depth), :], wv.at[p]) for p in range(parts)]
        x[:, :depth] = t0[...]
        x[:, depth:] = t1[...]
        for p in range(parts):
            fetches[p].wait()
            if p == 0:
                reads = fetch_slices()
            for j in range(total.shape[1]):
                total[p, j] = dot(x[...], wv[p, :, pl.ds(j * TILE, TILE)])
        for r in reads:
            r.wait()


def own_products(t0, t1, w, early, w_out):
    rows, depth = t0.shape
    parts, _, columns = w.shape
    shifts = (2, 1, -1, 0)
    return call(
        functools.partial(own_kernel, shifts),
        "own",
        (t0, t1, w, early, w_out),
        [like(F32, *early.shape), like(BF16, len(shifts), w_out.shape[0], 2 * depth)],
        12,
        4 * rows * depth * parts * columns,
        4 * depth * parts * columns + 2 * w_out.size,
        scratch=[
            pltpu.VMEM((rows, 2 * depth), BF16),
            pltpu.VMEM((parts, 2 * depth, columns), BF16),
            pltpu.SemaphoreType.DMA((parts + 1 + len(shifts),)),
        ],
        big=(2, 3, 4),
    )


def log_rows(log):
    high = log.astype(BF16).astype(F32)
    middle = (log - high).astype(BF16).astype(F32)
    low = log - high - middle
    row = lax.broadcasted_iota(jnp.int32, (LOG_ROWS, HD), 0)
    rows = jnp.where(row == 0, high, jnp.where(row == 1, middle, low))
    return jnp.where(row < 3, rows, 0.0).astype(BF16)


def log_of(message):
    tail = message[pl.ds(message.shape[0] - LOG_ROWS, LOG_ROWS), :].astype(F32)
    return jnp.minimum(tail[0:1] + tail[1:2] + tail[2:3], 0.0)


def send_order(n):
    return range(n - 1, 0, -1)


def place_along_y(n_y, shift=0):
    return lax.rem(lax.axis_index("seq") + (shift + n_y), n_y)


def key_value_kernel(n_y, f0, f1, w, total, ek, ends, shard, k_out, v_out, s1_out, *refs):
    messages, (x, scaled, sv) = refs[:n_y], refs[n_y:]
    n_tiles, rows, _ = k_out.shape
    depth = f0.shape[1]
    for i, f in enumerate((f0, f1)):
        x[:, i * depth : (i + 1) * depth] = f[...]
    group = n_tiles * 2 // n_y
    for i, out in enumerate((k_out, v_out)):
        for j in range(n_tiles):
            made = silu(total[i + 1, j] + dot(x[...], w[i + 1, :, pl.ds(j * TILE, TILE)])).astype(BF16)
            out[j] = made
            if i == 0:
                for b in range(2):
                    key = made[:, b * HD : (b + 1) * HD].astype(F32)
                    scaled[j, :, pl.ds(b * HD, HD)] = (key * ek[:, 2 * j + b : 2 * j + b + 1]).astype(BF16)
                continue
            both = []
            for c in range(rows // CHUNK):
                sl = pl.ds(c * CHUNK, CHUNK)
                both.append(
                    lax.dot_general(
                        scaled[j, sl, :], out[j, sl, :], (((0,), (0,)), ((), ())), preferred_element_type=F32
                    )
                )
            for b in range(2):
                h = 2 * j + b
                one = slice(b * HD, (b + 1) * HD)
                sums = [m[one, one] for m in both]
                s1_out[pl.ds(h * HD, HD), :] = sums[0]
                sv[h // group, pl.ds(h % group * HD, HD), :] = (
                    sums[0] * ends[1:2, h : h + 1] + sums[1]
                ).astype(BF16)
    for p in range(n_y):
        log = shard[...] if p == 0 else pltpu.roll(shard[...], HD - p * group, 1)
        sv[p, pl.ds(group * HD, LOG_ROWS), :] = log_rows(log)
    for d in range(n_y):
        messages[d][...] = sv[place_along_y(n_y, d)]


def key_value(n_y, far, w, total, ek, ends, shard):
    _, n_tiles, rows, _ = total.shape
    width = w.shape[2]
    depth = far[0].shape[1]
    size = (width // n_y + LOG_ROWS, HD)
    tiles = like(BF16, n_tiles, rows, TILE)
    return call(
        functools.partial(key_value_kernel, n_y),
        "key_value",
        (*far, w, total, ek, ends, shard),
        [tiles, tiles, like(F32, width, HD)] + [like(BF16, *size)] * n_y,
        16,
        4 * rows * 2 * depth * width,
        8 * rows * width + 8 * depth * width,
        scratch=[
            pltpu.VMEM((rows, 2 * depth), BF16),
            pltpu.VMEM((n_tiles, rows, TILE), BF16),
            pltpu.VMEM((n_y, *size), BF16),
        ],
    )


def query_kernel(f0, f1, w, total, q_out, x):
    depth = f0.shape[1]
    for i, f in enumerate((f0, f1)):
        x[:, i * depth : (i + 1) * depth] = f[...]
    for j in range(q_out.shape[0]):
        q_out[j] = silu(total[0, j] + dot(x[...], w[0, :, pl.ds(j * TILE, TILE)])).astype(BF16)


def query(far, w, total):
    _, n_tiles, rows, _ = total.shape
    depth = 2 * far[0].shape[1]
    return call(
        query_kernel,
        "query",
        (*far, w, total),
        [like(BF16, n_tiles, rows, TILE)],
        12,
        2 * rows * depth * n_tiles * TILE,
        6 * rows * n_tiles * TILE,
        scratch=[pltpu.VMEM((rows, depth), BF16)],
    )[0]


def inner_kernel(q, k, v, acol, arow, ea, qs_out, o_out, mark):
    mark[...] = jnp.zeros_like(mark)
    n_tiles, rows, _ = q.shape
    t = lax.broadcasted_iota(jnp.int32, (CHUNK, CHUNK), 0)
    s = lax.broadcasted_iota(jnp.int32, (CHUNK, CHUNK), 1)
    causal = s <= t
    for j in range(n_tiles):
        for b in range(2):
            h = 2 * j + b
            one = pl.ds(b * HD, HD)
            for c in range(rows // CHUNK):
                sl = pl.ds(c * CHUNK, CHUNK)
                scores = lax.dot_general(
                    q[j, sl, one], k[j, sl, one], (((1,), (1,)), ((), ())), preferred_element_type=F32
                )
                spread = acol[sl, h : h + 1] - arow[h : h + 1, sl]
                weighted = jnp.where(causal, scores * jnp.exp(jnp.minimum(spread, 0.0)), 0.0)
                o_out[j, sl, one] = dot(weighted.astype(BF16), v[j, sl, one])
                qs_out[j, sl, one] = (q[j, sl, one].astype(F32) * ea[sl, h : h + 1]).astype(BF16)


def inner(q, k, v, acol, arow, ea):
    n_tiles, rows, _ = k.shape
    tiles = (n_tiles, rows, TILE)
    return call(
        inner_kernel,
        "inner",
        (q, k, v, acol, arow, ea),
        [like(BF16, *tiles), like(F32, *tiles), MARK],
        16,
        4 * rows * CHUNK * n_tiles * TILE,
        14 * rows * n_tiles * TILE,
    )


def sum_logs(choose, logs):
    total = jnp.zeros_like(logs[0])
    for y, log in enumerate(logs):
        total = total + jnp.where(choose(y), log, 0.0)
    return total


def row_kernel(n_y, *refs):
    messages, (mark, out, done) = refs[:n_y], refs[n_y:]
    done[...] = mark[...]
    at = [place_along_y(n_y, -d) for d in (0, *send_order(n_y))]
    logs = [log_of(m) for m in messages]
    weights = [jnp.exp(sum_logs(lambda e: at[e] > at[d], logs)) for d in range(n_y)]
    for h in range(out.shape[0] // HD):
        one = pl.ds(h * HD, HD)
        total = None
        for weight, m in zip(weights, messages):
            term = m[one, :].astype(F32) * weight[:, h : h + 1]
            total = term if total is None else total + term
        out[one, :] = total.astype(BF16)
    out[pl.ds(out.shape[0] - LOG_ROWS, LOG_ROWS), :] = log_rows(sum(logs[1:], logs[0]))


def row_sum(messages, after):
    size = messages[0].shape
    n = len(messages)
    return call(
        functools.partial(row_kernel, n),
        "row_sum",
        (*messages, after),
        [like(BF16, *size), MARK],
        4,
        8 * size[0] * HD,
        16 * size[0] * HD,
    )


def state_kernel(n_y, n_z, *refs):
    messages, earlier, outs = refs[:n_y], refs[n_y : n_y + n_z - 1], refs[n_y + n_z :]
    my_z = lax.axis_index("seq") // n_y
    at = [place_along_y(n_y, -d) for d in (0, *send_order(n_y))]
    logs = [log_of(m) for m in messages]
    gap = jnp.zeros_like(logs[0])
    from_rows = []
    earlier = earlier[::-1]
    for e in range(1, n_z):
        from_rows.append(jnp.where(e <= my_z, jnp.exp(gap), 0.0))
        gap = gap + log_of(earlier[e - 1])
    for d in range(n_y):
        there = place_along_y(n_y, d)
        start = jnp.exp(sum_logs(lambda e: at[e] < there, logs))
        weights = [
            jnp.where(at[s] < there, jnp.exp(sum_logs(lambda e: (at[e] > at[s]) & (at[e] < there), logs)), 0.0)
            for s in range(n_y)
        ]
        for h in range(outs[d].shape[0] // HD):
            one = pl.ds(h * HD, HD)
            state = jnp.zeros((HD, HD), F32)
            for weight, m in zip(from_rows, earlier):
                state = state + m[one, :].astype(F32) * (weight[:, h : h + 1] * start[:, h : h + 1])
            for weight, m in zip(weights, messages):
                state = state + m[one, :].astype(F32) * weight[:, h : h + 1]
            outs[d][one, :] = state.astype(BF16)


def states(messages, earlier, after):
    n_y, n_z = len(messages), len(earlier) + 1
    rows = messages[0].shape[0] - LOG_ROWS
    return call(
        functools.partial(state_kernel, n_y, n_z),
        "states",
        (*messages, *earlier, after),
        [like(BF16, rows, HD)] * n_y,
        4,
        64 * rows * HD,
        24 * rows * HD,
    )


def attend_kernel(n_y, qs, o, w, s1, ends, *refs):
    received, (attn, top, bot, state) = refs[:n_y], refs[n_y:]
    half, slice_width = top.shape
    n_tiles = qs.shape[0]
    size = received[0].shape[0]
    for d, block in zip((0, *send_order(n_y)), received):
        row = pl.multiple_of(place_along_y(n_y, -d) * size, HD)
        state[pl.ds(row, size), :] = block[...]
    for j in range(n_tiles):
        for b in range(2):
            h = 2 * j + b
            cols = pl.ds(h * HD, HD)
            one = pl.ds(b * HD, HD)
            first = state[cols, :]
            second = (first.astype(F32) * ends[0:1, h : h + 1] + s1[cols, :]).astype(BF16)
            for c, held in ((0, first), (1, second)):
                sl = pl.ds(c * CHUNK, CHUNK)
                out = o[j, sl, one] + dot(qs[j, sl, one], held)
                mean = jnp.mean(out * out, axis=1, keepdims=True)
                attn[sl, cols] = (out * lax.rsqrt(mean + 1e-6)).astype(BF16)
    for j in range(slice_width // TILE):
        cols = pl.ds(j * TILE, TILE)
        out = dot(attn[...], w[0, :, cols]).astype(BF16)
        top[:, cols] = out[:half]
        bot[:, cols] = out[half:]


def attend(n_y, qs, o, w_out, s1, ends, received, slice_width):
    n_tiles, rows, _ = qs.shape
    width = n_tiles * TILE
    half = rows // 2
    return call(
        functools.partial(attend_kernel, n_y),
        "attend",
        (qs, o, w_out, s1, ends, *received),
        [like(BF16, rows, width), like(BF16, half, slice_width), like(BF16, half, slice_width)],
        16,
        2 * rows * width * (HD + slice_width),
        rows * width * 8 + width * slice_width * 2,
        scratch=[pltpu.VMEM((width, HD), BF16)],
    )


def columns_kernel(takes, attn, w, *refs):
    for (m, start, rows), out in zip(takes, refs):
        for j in range(out.shape[1] // TILE):
            cols = pl.ds(j * TILE, TILE)
            out[:, cols] = dot(attn[pl.ds(start, rows), :], w[m, :, cols]).astype(BF16)


def columns(takes, attn, w):
    slice_width = w.shape[2]
    rows = sum(r for _, _, r in takes)
    return call(
        functools.partial(columns_kernel, takes),
        "columns",
        (attn, w),
        [like(BF16, r, slice_width) for _, _, r in takes],
        16,
        2 * rows * attn.shape[1] * slice_width,
        6 * attn.shape[1] * slice_width + 2 * rows * slice_width,
    )


def finish_kernel(half, *refs):
    own, a, b, out, held, sem = (*refs[:3], *refs[-3:])
    rows = a.shape[0]
    sl = pl.ds(half * rows, rows)
    held[...] = (own[sl, :].astype(F32) + a[...].astype(F32) + b[...].astype(F32)).astype(BF16)
    copy = pltpu.make_async_copy(held, out.at[sl, :], sem)
    copy.start()
    copy.wait()


def finish(half, own, a, b, out=None):
    return call(
        functools.partial(finish_kernel, half),
        "finish",
        (own, a, b) if out is None else (own, a, b, out),
        [like(BF16, *own.shape)],
        8,
        own.size,
        own.size * 4,
        scratch=[pltpu.VMEM(a.shape, BF16), pltpu.SemaphoreType.DMA],
        big=(3,),
        big_outs=(0,),
        aliases=None if out is None else {3: 0},
    )[0]


def body(n_y, tokens, w_qkv, log_decay, w_out):
    slice_width = tokens.shape[1]
    n_t = lax.axis_size("tensor")
    n_z = lax.axis_size("seq") // n_y

    def along_x(x, shift):
        return lax.ppermute(x, "tensor", [(i, (i + shift) % n_t) for i in range(n_t)])

    def along_y(x, shift):
        return lax.ppermute(
            x, "seq", [(z * n_y + y, z * n_y + (y + shift) % n_y) for z in range(n_z) for y in range(n_y)]
        )

    def along_z(x, shift):
        return lax.ppermute(
            x, "seq", [(z * n_y + y, (z + shift) % n_z * n_y + y) for z in range(n_z) for y in range(n_y)]
        )

    w = w_qkv.transpose(1, 0, 2)
    t0, t1, early = split(tokens, w)

    l0 = along_x(t0, 1)
    r1 = along_x(t1, -1)
    l1 = along_x(t1, 1)
    r0 = along_x(t0, -1)
    f0 = along_x(l0, 1)
    f1 = along_x(r1, -1)

    far_places = ((2, 0), (2, 1))
    side_places = ((-1, 1), (1, 0))
    total, w_slices = own_products(t0, t1, w, early, w_out)
    total, w_side = near(((-1, 0), (1, 1)), (l0, r1), w, total, ahead=side_places)
    total, w_far = near(side_places, (l1, r0), w, total, w_side, ahead=far_places)
    arow, acol, ek, ea, ends, shard = decays(log_decay, total)
    far = (f0, f1)
    k, v, s1, *kvs = key_value(n_y, far, w_far, total, ek, ends, shard)

    sums = [kvs[0]] + [along_y(kvs[d], d) for d in send_order(n_y)]
    q = query(far, w_far, total)
    qs, o, mark = inner(q, k, v, acol, arow, ea)
    row, mark = row_sum(sums, mark)
    earlier = [along_z(row, e) for e in send_order(n_z)]
    starts = states(sums, earlier, mark)
    received = [starts[0]] + [along_y(starts[d], d) for d in send_order(n_y)]

    attn, far_top, far_bot = attend(n_y, qs, o, w_slices, s1, ends, received, slice_width)
    relay_top = along_x(far_top, 1)
    relay_bot = along_x(far_bot, -1)
    rows, half = attn.shape[0], attn.shape[0] // 2
    p_bot, m_top = columns([(1, half, half), (2, 0, half)], attn, w_slices)
    left_bot = along_x(p_bot, 1)
    right_top = along_x(m_top, -1)
    p_top, m_bot, own = columns([(1, 0, half), (2, half, half), (3, 0, rows)], attn, w_slices)
    left_top = along_x(p_top + relay_top, 1)
    right_bot = along_x(m_bot + relay_bot, -1)
    out = finish(1, own, left_bot, right_bot)
    return finish(0, own, left_top, right_top, out)


def solution(mesh):
    in_specs = (
        P(("dp", "seq"), "tensor"),
        P(None, None, "tensor"),
        P("tensor", ("dp", "seq")),
        P("tensor", None),
    )
    out_specs = P(("dp", "seq"), "tensor")
    n_seq = mesh.shape["seq"]
    n_y = 4 if n_seq % 4 == 0 else 1
    return jax.shard_map(
        functools.partial(body, n_y), mesh=mesh, in_specs=in_specs, out_specs=out_specs, check_vma=False
    )
```
